512 devices in a mesh: ctx: 8 (over x, core), dp: 8 (over y), mp: 8 (over z).
Axes of the slice: x: 4, y: 8, z: 8, core: 2. Of those that a mesh axis runs over, the one named last changes fastest.
Arguments:
- queries: bfloat16 [16384, 5120], P(('ctx', 'dp'), 'mp'), may hold values from -200 to 200, as said below
- suffix_keys: bfloat16 [16384, 1024], P(('ctx', 'dp'), 'mp'), may hold values from -6 to 6
- suffix_values: bfloat16 [16384, 1024], P(('ctx', 'dp'), 'mp'), may hold values from -6 to 6
- pre_keys: bfloat16 [3072, 1024], P('ctx', 'mp'), may hold values from -6 to 6
- pre_values: bfloat16 [3072, 1024], P('ctx', 'mp'), may hold values from -6 to 6
- segments: int32 [64, 256], P(('ctx', 'dp')), may hold values from 0 to 7, never falling along the last dimension, each value on 1 to 64 neighbouring positions
- d_out: bfloat16 [16384, 5120], P(('ctx', 'dp'), 'mp'), may hold values from -6 to 6
Outputs:
- attended: bfloat16 [16384, 5120], P(('ctx', 'dp'), 'mp')
- d_queries: bfloat16 [16384, 5120], P(('ctx', 'dp'), 'mp')
- suffix_keys_gradient: bfloat16 [16384, 1024], P(('ctx', 'dp'), 'mp')
- suffix_values_gradient: bfloat16 [16384, 1024], P(('ctx', 'dp'), 'mp')
- d_pre_keys: float32 [3072, 1024], P(('ctx', 'dp'), 'mp')
- d_pre_values: float32 [3072, 1024], P(('ctx', 'dp'), 'mp')
The draws below stay inside these ranges and needn't reach their ends.
Inputs may be any that keep to these rules, and one draw needn't show every extreme that they name: `queries`: scaled Gaussian entries.
All inputs are finite; a program needn't handle non-finite values.
Results may differ from the reference program's by a relative error of at most 0.023.
Values may be sent and summed in bfloat16 or wider, within the bound.
A program may use at most 64 MiB of HBM per device.

```python
import math
import jax
import jax.numpy as jnp
import numpy as np
from jax import lax

HEAD_WIDTH = 128
Q_HEADS = 40
KEY_VALUE_HEADS = 8
SUFFIX_PER_SHARD = 256
QUESTIONS = 8
MOST = 64
QUESTION_BLOCKS = 64
PREFIX = 3072
SUFFIX_TOKENS = 16384


def draw_queries(key, part):
    key = jax.random.fold_in(key, 5)
    base = jax.random.normal(jax.random.fold_in(key, 1), (SUFFIX_TOKENS, Q_HEADS * HEAD_WIDTH), jnp.float32)
    return jnp.clip(base, -6.0, 6.0).astype(jnp.bfloat16)


def block_levels(key, extent, cuts, smallest, largest):
    loudness = 1.0
    for dim, parts in cuts:
        heights = jax.random.uniform(jax.random.fold_in(jax.random.fold_in(key, 6), dim), (parts,), jnp.float32, smallest / len(cuts), largest / len(cuts))
        loudness = loudness * jnp.repeat(jnp.exp(heights), extent[dim] // parts).reshape((-1,) + (1,) * (len(extent) - 1 - dim))
    return loudness


def profile(number_of, total, bound, skew):
    loads = [(1 << 20) // math.isqrt(rank ** skew) + 1 for rank in range(2, number_of + 1)]
    surplus, holding = total - bound - (number_of - 1), [1] * (number_of - 1)
    while surplus > 0:
        free = [i for i in range(number_of - 1) if holding[i] < bound]
        mass, left = sum([loads[i] for i in free]), surplus
        for i in free:
            extra = min(bound - holding[i], max(1, left * loads[i] // mass), surplus)
            holding[i] = holding[i] + extra
            surplus = surplus - extra
    return np.array([bound] + holding)


def ragged_sizes(rng, count, total, bound, slope):
    if count == 2:
        one = jax.random.randint(rng, (), max(1, total - bound), min(bound, total - 1) + 1)
        return jnp.stack([one, total - one])
    tallies = jnp.asarray(profile(count, total, bound, slope), jnp.int32)
    couples = (count - 1) // 2
    giver, taker = tallies[1:1 + 2 * couples:2], tallies[2:2 + 2 * couples:2]
    margin = jnp.minimum(giver - 1, bound - taker)
    moved = jax.random.randint(jax.random.fold_in(rng, 1), (couples,), 0, 1 << 20) % (margin + 1)
    tallies = tallies.at[1:1 + 2 * couples:2].set(giver - moved).at[2:2 + 2 * couples:2].set(taker + moved)
    return tallies[jax.random.permutation(jax.random.fold_in(rng, 2), count)]


def scatter_about(rng, extent, width, limit, cuts=(), dtype=jnp.bfloat16):
    drawn = width * jax.random.normal(rng, extent, jnp.float32)
    if cuts:
        drawn = drawn * block_levels(rng, extent, cuts, -0.22, 0.18)
    return jnp.clip(drawn, -limit, limit).astype(dtype)


def setup_inputs(seed: int = 0) -> dict:
    arg_keys = jax.random.split(jax.random.key(seed), 8)
    queries = draw_queries(jax.random.fold_in(arg_keys[7], 71), 0)
    suffix_keys = scatter_about(arg_keys[1], (SUFFIX_TOKENS, KEY_VALUE_HEADS * HEAD_WIDTH), 1.0, 6.0, ((0, 64), (1, 8)))
    suffix_values = scatter_about(arg_keys[2], (SUFFIX_TOKENS, KEY_VALUE_HEADS * HEAD_WIDTH), 1.0, 6.0, ((0, 64), (1, 8)))
    pre_keys = scatter_about(arg_keys[3], (PREFIX, KEY_VALUE_HEADS * HEAD_WIDTH), 1.0, 6.0, ((0, 8), (1, 8)))
    pre_values = scatter_about(arg_keys[4], (PREFIX, KEY_VALUE_HEADS * HEAD_WIDTH), 1.0, 6.0, ((0, 8), (1, 8)))
    segments = jax.vmap(lambda own: jnp.searchsorted(jnp.cumsum(ragged_sizes(own, QUESTIONS, SUFFIX_PER_SHARD, MOST, 2)), jnp.arange(SUFFIX_PER_SHARD), side="right"))(jax.random.split(arg_keys[5], QUESTION_BLOCKS)).reshape((QUESTION_BLOCKS, SUFFIX_PER_SHARD)).astype(jnp.int32)
    d_out = scatter_about(arg_keys[6], (SUFFIX_TOKENS, Q_HEADS * HEAD_WIDTH), 1.0, 6.0, ((0, 64), (1, 8)))
    return {"queries": queries, "suffix_keys": suffix_keys, "suffix_values": suffix_values, "pre_keys": pre_keys, "pre_values": pre_values, "segments": segments, "d_out": d_out}


def reference(queries, suffix_keys, suffix_values, pre_keys, pre_values, segments, d_out):
    per_group = Q_HEADS // KEY_VALUE_HEADS
    att_scale = HEAD_WIDTH ** -0.5
    prefix_key_rows = pre_keys.reshape(PREFIX, KEY_VALUE_HEADS, HEAD_WIDTH)
    prefix_value_rows = pre_values.reshape(PREFIX, KEY_VALUE_HEADS, HEAD_WIDTH)
    query_block = queries.reshape(QUESTION_BLOCKS, SUFFIX_PER_SHARD, KEY_VALUE_HEADS, per_group, HEAD_WIDTH)
    output_gradient_block = d_out.reshape(QUESTION_BLOCKS, SUFFIX_PER_SHARD, KEY_VALUE_HEADS, per_group, HEAD_WIDTH)
    suffix_key_block = suffix_keys.reshape(QUESTION_BLOCKS, SUFFIX_PER_SHARD, KEY_VALUE_HEADS, HEAD_WIDTH)
    suffix_value_block = suffix_values.reshape(QUESTION_BLOCKS, SUFFIX_PER_SHARD, KEY_VALUE_HEADS, HEAD_WIDTH)
    row_ids = lax.broadcasted_iota(jnp.int32, (SUFFIX_PER_SHARD, SUFFIX_PER_SHARD), 0)
    col_ids = lax.broadcasted_iota(jnp.int32, (SUFFIX_PER_SHARD, SUFFIX_PER_SHARD), 1)

    def single_block(carry, block_entries):
        query_rows, suffix_key_rows, suffix_value_rows, segment_index, output_gradient = block_entries
        joined_keys = jnp.concatenate([prefix_key_rows, suffix_key_rows], 0).astype(jnp.float32)
        joined_values = jnp.concatenate([prefix_value_rows, suffix_value_rows], 0).astype(jnp.float32)
        quer_f = query_rows.astype(jnp.float32)
        dout_f = output_gradient.astype(jnp.float32)
        local_ok = (segment_index[:, None] == segment_index[None, :]) & (col_ids <= row_ids)
        allowed = jnp.concatenate([jnp.ones((SUFFIX_PER_SHARD, PREFIX), bool), local_ok], 1)
        scores = jnp.einsum('ihgd,jhd->hgij', quer_f, joined_keys) * att_scale
        scores = jnp.where(allowed[None, None], scores, -1e30)
        top = jnp.max(scores, -1, keepdims=True)
        expo = jnp.exp(scores - top)
        weights = expo / jnp.sum(expo, -1, keepdims=True)
        weights_bf = lax.optimization_barrier(weights.astype(jnp.bfloat16)).astype(jnp.float32)
        out = jnp.einsum('hgij,jhd->ihgd', weights_bf, joined_values)
        delta = jnp.einsum('ihgd,ihgd->hgi', dout_f, out)
        d_weights = jnp.einsum('ihgd,jhd->hgij', dout_f, joined_values)
        d_scores = lax.optimization_barrier((weights * (d_weights - delta[..., None])).astype(jnp.bfloat16)).astype(jnp.float32)
        query_gradient = jnp.einsum('hgij,jhd->ihgd', d_scores, joined_keys) * att_scale
        d_key = jnp.einsum('hgij,ihgd->jhd', d_scores, quer_f) * att_scale
        d_val = jnp.einsum('hgij,ihgd->jhd', weights_bf, dout_f)
        new_carry = (carry[0] + d_key[:PREFIX], carry[1] + d_val[:PREFIX])
        results = (out.astype(jnp.bfloat16), query_gradient.astype(jnp.bfloat16),
                   d_key[PREFIX:].astype(jnp.bfloat16), d_val[PREFIX:].astype(jnp.bfloat16))
        return new_carry, results

    block_offset = (jnp.zeros((PREFIX, KEY_VALUE_HEADS, HEAD_WIDTH), jnp.float32), jnp.zeros((PREFIX, KEY_VALUE_HEADS, HEAD_WIDTH), jnp.float32))
    (key_gradient_total, value_gradient_total), (output_blocks, query_gradient, suffix_key_gradient, suffix_value_gradient) = lax.scan(single_block, block_offset, (query_block, suffix_key_block, suffix_value_block, segments, output_gradient_block))
    attended = output_blocks.reshape(SUFFIX_TOKENS, Q_HEADS * HEAD_WIDTH)
    d_queries = query_gradient.reshape(SUFFIX_TOKENS, Q_HEADS * HEAD_WIDTH)
    suffix_keys_gradient = suffix_key_gradient.reshape(SUFFIX_TOKENS, KEY_VALUE_HEADS * HEAD_WIDTH)
    suffix_values_gradient = suffix_value_gradient.reshape(SUFFIX_TOKENS, KEY_VALUE_HEADS * HEAD_WIDTH)
    d_pre_keys = key_gradient_total.reshape(PREFIX, KEY_VALUE_HEADS * HEAD_WIDTH)
    d_pre_values = value_gradient_total.reshape(PREFIX, KEY_VALUE_HEADS * HEAD_WIDTH)
    return (attended, d_queries, suffix_keys_gradient, suffix_values_gradient, d_pre_keys, d_pre_values)
```

```python
import jax
import jax.numpy as jnp
from jax import lax
from jax.experimental import pallas as pl
from jax.experimental.pallas import tpu as pltpu
from jax.sharding import PartitionSpec as P

HEAD_WIDTH = 128
HEADS = 5
TOKENS = 256
ROWS = HEADS * TOKENS
OWN = 384
PIECE = 48
SCALE = HEAD_WIDTH ** (-0.5)
LOG2_SCALE = 1.4426950408889634 * SCALE
MESH = pl.DeviceIdType.MESH
bf16 = jnp.bfloat16
f32 = jnp.float32

KEYS = TOKENS + 8 * OWN
SLOT = [TOKENS + OWN * i for i in range(8)]
CHUNKS = [(0, 640), (640, 384), (1024, 768), (1792, 768), (2560, 384), (2944, 384)]
CHUNK_OF_SLOT = [0, 1, 2, 2, 3, 3, 4, 5]
STRIP = 256


def dot(left, right):
    return lax.dot_general(left, right, (((1,), (0,)), ((), ())), preferred_element_type=f32)


def head_cols(head):
    return slice(head * TOKENS, (head + 1) * TOKENS)


def strips(count):
    return [(at, min(STRIP, count - at)) for at in range(0, count, STRIP)]


def kernel(
    q_ref, sk_ref, sv_ref, pk_ref, pv_ref, seg_ref, do_ref,
    out_ref, dq_ref, dsk_ref, dsv_ref, dpk_ref, dpv_ref,
    kv, qT, dT, qs, ds, kT, vT, k2, bias, top, total, acc, tops, delta, factor, s_buf, p_buf, d_buf,
    keep, sib_send, sib_recv, x_send, x_recv, y_send, y_recv,
    ag_s, ag_r, sib_s, sib_r, x_s, x_r, y_s, y_r,
):
    ctx = lax.axis_index("ctx")
    dp = lax.axis_index("dp")
    core = ctx % 2
    chip = ctx // 2
    ahead = ((chip + 1 + 2 * core) % 4) * 2 + core
    behind = ((chip + 3 + 2 * core) % 4) * 2 + core
    other = chip * 2 + (1 - core)

    barrier = pltpu.get_barrier_semaphore()
    for peer in (ahead, behind, other):
        pl.semaphore_signal(barrier, inc=1, device_id={"ctx": peer}, device_id_type=MESH)
    for step in range(1, 8):
        pl.semaphore_signal(barrier, inc=1, device_id={"dp": (dp + step) % 8}, device_id_type=MESH)

    def send(src, dst, s_sem, r_sem, device):
        copy = pltpu.make_async_remote_copy(
            src_ref=src, dst_ref=dst, send_sem=s_sem, recv_sem=r_sem, device_id=device, device_id_type=MESH
        )
        copy.start()
        return copy

    def spread(index, source, slot, peer):
        return send(kv.at[source], kv.at[slot], ag_s.at[index], ag_r.at[slot], {"ctx": peer})

    def arrived(slot):
        pltpu.make_async_remote_copy(
            src_ref=kv.at[slot], dst_ref=kv.at[slot], send_sem=ag_s.at[0], recv_sem=ag_r.at[slot],
            device_id={"ctx": other}, device_id_type=MESH,
        ).wait_recv()

    def prepare_keys(start, keys, values):
        count = keys.shape[0]
        kT[:, start:start + count] = keys.T
        vT[0:128, start:start + count] = values.T
        scaled = keys.astype(f32) * LOG2_SCALE
        high = scaled.astype(bf16)
        k2[start:start + count, 0:128] = high
        k2[start:start + count, 128:256] = (scaled - high.astype(f32)).astype(bf16)

    kv[0, 0] = pk_ref[...]
    kv[0, 1] = pv_ref[...]
    pl.semaphore_wait(barrier, 10)
    sends = [spread(0, 0, 3, ahead), spread(1, 0, 2, behind), spread(2, 0, 1, other)]

    for head in range(HEADS):
        cols = head_cols(head)
        width = slice(head * 128, (head + 1) * 128)
        q_head, do_head = q_ref[:, width], do_ref[:, width]
        q_turned = q_head.T
        qT[0:128, cols] = q_turned
        qT[128:256, cols] = q_turned
        dT[:, cols] = do_head.T
        qs[cols, :] = q_head
        ds[cols, :] = do_head
    seg = jnp.broadcast_to(seg_ref[...].astype(f32), (TOKENS, TOKENS))
    key_id = lax.broadcasted_iota(jnp.int32, (TOKENS, TOKENS), 0)
    token_id = lax.broadcasted_iota(jnp.int32, (TOKENS, TOKENS), 1)
    bias[...] = jnp.where((seg == seg.T) & (key_id <= token_id), 0.0, -1e30)
    vT[128:144, :] = jnp.where(lax.broadcasted_iota(jnp.int32, (16, KEYS), 0) == 0, 1.0, 0.0).astype(bf16)
    prepare_keys(0, sk_ref[...], sv_ref[...])
    prepare_keys(SLOT[0], pk_ref[...], pv_ref[...])

    def ready(slot):
        prepare_keys(SLOT[slot], kv[slot, 0], kv[slot, 1])

    def before_chunk(chunk):
        if chunk == 1:
            arrived(1)
            ready(1)
        if chunk == 2:
            arrived(3)
            sends.append(spread(3, 3, 6, ahead))
            sends.append(spread(4, 3, 4, other))
            arrived(2)
            sends.append(spread(5, 2, 5, other))
            ready(2)
            ready(3)
        if chunk == 3:
            arrived(4)
            arrived(5)
            ready(4)
            ready(5)
        if chunk == 4:
            arrived(6)
            sends.append(spread(6, 6, 7, other))
            ready(6)
        if chunk == 5:
            arrived(7)
            ready(7)

    steps = [(chunk, head) for chunk in range(len(CHUNKS)) for head in range(HEADS)]
    peak, fade = {}, {}

    def score_strip(index, at, count):
        chunk, head = steps[index]
        start = CHUNKS[chunk][0] + at
        s = dot(k2[start:start + count, :], qT[:, head_cols(head)])
        if chunk == 0 and at < TOKENS:
            s = s + bias[at:at + count, :]
        s_buf[index % 2, at:at + count, :] = s
        part = jnp.max(s.reshape(count // 8, 8, TOKENS), 0)
        peak[index] = part if index not in peak else jnp.maximum(peak[index], part)

    def finish_peak(index):
        chunk, head = steps[index]
        cols = head_cols(head)
        highest = jnp.max(peak[index], 0, keepdims=True)
        if chunk > 0:
            before = top[:, cols]
            highest = jnp.maximum(highest, before)
            fade[index] = jnp.exp2(before - highest)
        top[:, cols] = highest
        tops[chunk:chunk + 1, cols] = highest
        peak[index] = highest

    def weight_strip(index, at, count):
        chunk, head = steps[index]
        start = CHUNKS[chunk][0] + at
        p_buf[start:start + count, head_cols(head)] = jnp.exp2(
            s_buf[index % 2, at:at + count, :] - peak[index]
        ).astype(bf16)

    def gather_values(index):
        chunk, head = steps[index]
        cols = head_cols(head)
        start, count = CHUNKS[chunk]
        found = dot(vT[:, start:start + count], p_buf[start:start + count, cols])
        if chunk > 0:
            total[:, cols] = total[:, cols] * fade[index] + found[128:129]
            acc[:, cols] = acc[:, cols] * fade[index] + found[:128]
        else:
            total[:, cols] = found[128:129]
            acc[:, cols] = found[:128]

    for at, count in strips(CHUNKS[0][1]):
        score_strip(0, at, count)
    for index in range(len(steps)):
        finish_peak(index)
        now = strips(CHUNKS[steps[index][0]][1])
        later = []
        if index + 1 < len(steps):
            chunk = steps[index + 1][0]
            if chunk != steps[index][0]:
                before_chunk(chunk)
            later = strips(CHUNKS[chunk][1])
        for turn in range(max(len(now), len(later))):
            if turn < len(later):
                score_strip(index + 1, *later[turn])
            if turn < len(now):
                weight_strip(index, *now[turn])
            if turn == 0 and index > 0:
                gather_values(index - 1)
    gather_values(len(steps) - 1)

    for head in range(HEADS):
        cols = head_cols(head)
        inverse = 1.0 / total[:, cols]
        out = acc[:, cols] * inverse
        delta[:, cols] = jnp.sum(out * dT[:, cols].astype(f32), 0, keepdims=True)
        out_ref[:, head * 128:(head + 1) * 128] = out.T.astype(bf16)
        for chunk in range(len(CHUNKS)):
            factor[chunk:chunk + 1, cols] = jnp.exp2(tops[chunk:chunk + 1, cols] - top[:, cols]) * inverse

    def back(start, count, chunk, values):
        for head in range(HEADS):
            cols = head_cols(head)
            weights = p_buf[start:start + count, cols] * factor[chunk:chunk + 1, cols].astype(bf16)
            p_buf[start:start + count, cols] = weights
            d_weights = dot(values, dT[:, cols])
            d_buf[start:start + count, cols] = weights * (d_weights - delta[:, cols]).astype(bf16)
        rows = slice(start, start + count)
        return dot(d_buf[rows, :], qs[...]) * SCALE, dot(p_buf[rows, :], ds[...])

    def back_slot(slot):
        return back(SLOT[slot], OWN, CHUNK_OF_SLOT[slot], kv[slot, 1])

    def to_other(index, slot):
        dk, dv = back_slot(slot)
        sib_send[index, :, 0:128] = dk.astype(bf16)
        sib_send[index, :, 128:256] = dv.astype(bf16)
        landing = {0: 0, 1: 2, 2: 1, 3: 3}[index]
        sends.append(
            send(sib_send.at[index], sib_recv.at[landing], sib_s.at[index], sib_r.at[landing], {"ctx": other})
        )

    def hold(index, slot):
        dk, dv = back_slot(slot)
        keep[index, :, 0:128] = dk
        keep[index, :, 128:256] = dv

    def landed(buffer, sems, index):
        pltpu.make_async_remote_copy(
            src_ref=buffer.at[index], dst_ref=buffer.at[index], send_sem=sems.at[index], recv_sem=sems.at[index],
            device_id={"ctx": other}, device_id_type=MESH,
        ).wait_recv()

    def to_chip(index, peer, value):
        x_send[index] = value.astype(bf16)
        sends.append(send(x_send.at[index], x_recv.at[index], x_s.at[index], x_r.at[index], {"ctx": peer}))

    def pair_sum(index):
        landed(sib_recv, sib_r, index)
        return keep[index] + sib_recv[index].astype(f32)

    to_other(0, 7)
    hold(0, 6)
    to_other(1, 4)
    to_other(2, 5)
    to_chip(0, ahead, pair_sum(0))
    hold(2, 3)
    hold(1, 2)
    to_chip(1, behind, pair_sum(2))
    to_other(3, 1)
    landed(x_recv, x_r, 0)
    to_chip(2, ahead, pair_sum(1) + x_recv[0].astype(f32))
    hold(3, 0)

    dk, dv = back(0, TOKENS, 0, sv_ref[...])
    dsk_ref[...] = dk.astype(bf16)
    dsv_ref[...] = dv.astype(bf16)

    def queries_gradient(head):
        turned = dot(kT[...], d_buf[:, head_cols(head)]) * SCALE
        dq_ref[:, head * 128:(head + 1) * 128] = turned.T.astype(bf16)

    queries_gradient(0)
    queries_gradient(1)
    keep[3] = pair_sum(3)
    landed(x_recv, x_r, 1)
    landed(x_recv, x_r, 2)
    keep[3] = keep[3] + x_recv[1].astype(f32) + x_recv[2].astype(f32)
    for piece in range(8):
        y_send[piece] = keep[3, piece * PIECE:(piece + 1) * PIECE, :].astype(bf16)
    for step in range(1, 8):
        peer = (dp + step) % 8
        sends.append(send(y_send.at[peer], y_recv.at[step], y_s.at[step], y_r.at[step], {"dp": peer}))
    for head in range(2, HEADS):
        queries_gradient(head)
    mine = keep[3, pl.ds(pl.multiple_of(dp * PIECE, 8), PIECE), :]
    for step in range(1, 8):
        landed(y_recv, y_r, step)
        mine = mine + y_recv[step].astype(f32)
    dpk_ref[...] = mine[:, 0:128]
    dpv_ref[...] = mine[:, 128:256]
    for copy in sends:
        copy.wait_send()


def shards(queries, suffix_keys, suffix_values, pre_keys, pre_values, segments, d_out):
    vmem = pl.BlockSpec(memory_space=pltpu.VMEM)
    dma = pltpu.SemaphoreType.DMA
    return pl.pallas_call(
        kernel,
        out_shape=[
            jax.ShapeDtypeStruct((TOKENS, HEADS * HEAD_WIDTH), bf16),
            jax.ShapeDtypeStruct((TOKENS, HEADS * HEAD_WIDTH), bf16),
            jax.ShapeDtypeStruct((TOKENS, HEAD_WIDTH), bf16),
            jax.ShapeDtypeStruct((TOKENS, HEAD_WIDTH), bf16),
            jax.ShapeDtypeStruct((PIECE, HEAD_WIDTH), f32),
            jax.ShapeDtypeStruct((PIECE, HEAD_WIDTH), f32),
        ],
        in_specs=[vmem] * 7,
        out_specs=[vmem] * 6,
        scratch_shapes=[
            pltpu.VMEM((8, 2, OWN, HEAD_WIDTH), bf16),
            pltpu.VMEM((256, ROWS), bf16),
            pltpu.VMEM((128, ROWS), bf16),
            pltpu.VMEM((ROWS, HEAD_WIDTH), bf16),
            pltpu.VMEM((ROWS, HEAD_WIDTH), bf16),
            pltpu.VMEM((128, KEYS), bf16),
            pltpu.VMEM((144, KEYS), bf16),
            pltpu.VMEM((KEYS, 256), bf16),
            pltpu.VMEM((TOKENS, TOKENS), f32),
            pltpu.VMEM((1, ROWS), f32),
            pltpu.VMEM((1, ROWS), f32),
            pltpu.VMEM((128, ROWS), f32),
            pltpu.VMEM((8, ROWS), f32),
            pltpu.VMEM((1, ROWS), f32),
            pltpu.VMEM((8, ROWS), f32),
            pltpu.VMEM((2, 768, TOKENS), f32),
            pltpu.VMEM((KEYS, ROWS), bf16),
            pltpu.VMEM((KEYS, ROWS), bf16),
            pltpu.VMEM((4, OWN, 256), f32),
            pltpu.VMEM((4, OWN, 256), bf16),
            pltpu.VMEM((4, OWN, 256), bf16),
            pltpu.VMEM((3, OWN, 256), bf16),
            pltpu.VMEM((3, OWN, 256), bf16),
            pltpu.VMEM((8, PIECE, 256), bf16),
            pltpu.VMEM((8, PIECE, 256), bf16),
            dma((7,)), dma((8,)), dma((4,)), dma((4,)), dma((3,)), dma((3,)), dma((8,)), dma((8,)),
        ],
        compiler_params=pltpu.CompilerParams(
            collective_id=0, has_side_effects=True, vmem_limit_bytes=60 << 20
        ),
    )(queries, suffix_keys, suffix_values, pre_keys, pre_values, segments, d_out)


def solution(mesh):
    split = P(("ctx", "dp"), "mp")
    in_specs = (split, split, split, P("ctx", "mp"), P("ctx", "mp"), P(("ctx", "dp"), None), split)
    return jax.shard_map(shards, mesh=mesh, in_specs=in_specs, out_specs=(split,) * 6, check_vma=False)
```

```python
import jax
import jax.numpy as jnp
from jax import lax
from jax.experimental import pallas as pl
from jax.experimental.pallas import tpu as pltpu
from jax.sharding import PartitionSpec as P

HEAD_WIDTH = 128
HEADS = 5
TOKENS = 256
ROWS = HEADS * TOKENS
OWN = 384
PIECE = 48
SCALE = HEAD_WIDTH ** (-0.5)
LOG2_SCALE = 1.4426950408889634 * SCALE
MESH = pl.DeviceIdType.MESH
bf16 = jnp.bfloat16
f32 = jnp.float32

PART = 128
PARTS = 3
ARRIVALS = [
    [(0, 0), (0, 1), (0, 2)],
    [(1, 0), (1, 1), (1, 2)],
    [(2, 0), (3, 0)],
    [(2, 1), (3, 1), (4, 0), (5, 0)],
    [(2, 2), (3, 2), (4, 1), (5, 1), (6, 0)],
    [(4, 2), (5, 2), (6, 1), (7, 0)],
    [(6, 2), (7, 1), (7, 2)],
]
KEYS = TOKENS + 8 * OWN
START, CHUNK_OF, CHUNKS = {}, {}, []
for chunk, arriving in enumerate(ARRIVALS):
    begin = 0 if chunk == 0 else sum(CHUNKS[-1])
    at = TOKENS if chunk == 0 else begin
    for place in arriving:
        START[place], CHUNK_OF[place] = at, chunk
        at += PART
    CHUNKS.append((begin, at - begin))
STRIP = 256
LANDING = {0: 0, 1: 2, 2: 1, 3: 3}


def dot(left, right):
    return lax.dot_general(left, right, (((1,), (0,)), ((), ())), preferred_element_type=f32)


def head_cols(head):
    return slice(head * TOKENS, (head + 1) * TOKENS)


def strips(count):
    return [(at, min(STRIP, count - at)) for at in range(0, count, STRIP)]


def kernel(
    q_ref, sk_ref, sv_ref, pk_ref, pv_ref, seg_ref, do_ref,
    out_ref, dq_ref, dsk_ref, dsv_ref, dpk_ref, dpv_ref,
    q_v, sk_v, sv_v, pk_v, pv_v, seg_v, do_v, out_v, dq_v, dsk_v, dsv_v, dpk_v, dpv_v,
    kv, qT, dT, qs, ds, kT, vT, k2, bias, top, total, acc, tops, delta, factor, s_buf, p_buf, d_buf,
    keep, sib_send, sib_recv, x_send, x_recv, y_send, y_recv,
    in_s, out_s, ag_s, ag_r, sib_s, sib_r, x_s, x_r, y_s, y_r,
):
    ctx = lax.axis_index("ctx")
    dp = lax.axis_index("dp")
    core = ctx % 2
    chip = ctx // 2
    ahead = ((chip + 1 + 2 * core) % 4) * 2 + core
    behind = ((chip + 3 + 2 * core) % 4) * 2 + core
    other = chip * 2 + (1 - core)

    barrier = pltpu.get_barrier_semaphore()
    for peer in (ahead, behind, other):
        pl.semaphore_signal(barrier, inc=1, device_id={"ctx": peer}, device_id_type=MESH)
    for step in range(1, 8):
        pl.semaphore_signal(barrier, inc=1, device_id={"dp": (dp + step) % 8}, device_id_type=MESH)

    loads = {}
    for index, (name, source, target) in enumerate((
        ("pk", pk_ref, pk_v), ("pv", pv_ref, pv_v), ("q", q_ref, q_v), ("seg", seg_ref, seg_v),
        ("sk", sk_ref, sk_v), ("sv", sv_ref, sv_v), ("do", do_ref, do_v),
    )):
        loads[name] = pltpu.make_async_copy(source, target, in_s.at[index])
        loads[name].start()
    stores = []

    def store(source, target):
        copy = pltpu.make_async_copy(source, target, out_s.at[len(stores)])
        copy.start()
        stores.append(copy)

    sends = []

    def send(src, dst, s_sem, r_sem, device):
        copy = pltpu.make_async_remote_copy(
            src_ref=src, dst_ref=dst, send_sem=s_sem, recv_sem=r_sem, device_id=device, device_id_type=MESH
        )
        copy.start()
        sends.append(copy)

    counter = []

    def spread(source, slot, part, peer):
        index = len(counter)
        counter.append(0)
        send(kv.at[source, part], kv.at[slot, part], ag_s.at[index], ag_r.at[slot, part], {"ctx": peer})

    def arrived(slot, part):
        pltpu.make_async_remote_copy(
            src_ref=kv.at[slot, part], dst_ref=kv.at[slot, part], send_sem=ag_s.at[0], recv_sem=ag_r.at[slot, part],
            device_id={"ctx": other}, device_id_type=MESH,
        ).wait_recv()

    def prepare_keys(start, keys, values):
        count = keys.shape[0]
        kT[:, start:start + count] = keys.T
        vT[0:128, start:start + count] = values.T
        scaled = keys.astype(f32) * LOG2_SCALE
        high = scaled.astype(bf16)
        k2[start:start + count, 0:128] = high
        k2[start:start + count, 128:256] = (scaled - high.astype(f32)).astype(bf16)

    def ready(slot, part):
        prepare_keys(START[slot, part], kv[slot, part, 0], kv[slot, part, 1])

    loads["pk"].wait()
    loads["pv"].wait()
    for part in range(PARTS):
        for owner in range(8):
            rows = slice(owner * PIECE + part * 16, owner * PIECE + part * 16 + 16)
            kv[0, part, 0, owner * 16:owner * 16 + 16, :] = pk_v[rows, :]
            kv[0, part, 1, owner * 16:owner * 16 + 16, :] = pv_v[rows, :]
    pl.semaphore_wait(barrier, 10)
    for part in range(PARTS):
        spread(0, 3, part, ahead)
        spread(0, 2, part, behind)
        spread(0, 1, part, other)

    loads["q"].wait()
    loads["seg"].wait()
    loads["sk"].wait()
    loads["sv"].wait()
    loads["do"].wait()
    for head in range(HEADS):
        cols = head_cols(head)
        width = slice(head * 128, (head + 1) * 128)
        q_head, do_head = q_v[:, width], do_v[:, width]
        q_turned = q_head.T
        qT[0:128, cols] = q_turned
        qT[128:256, cols] = q_turned
        dT[:, cols] = do_head.T
        qs[cols, :] = q_head
        ds[cols, :] = do_head
    seg = jnp.broadcast_to(seg_v[...].astype(f32), (TOKENS, TOKENS))
    key_id = lax.broadcasted_iota(jnp.int32, (TOKENS, TOKENS), 0)
    token_id = lax.broadcasted_iota(jnp.int32, (TOKENS, TOKENS), 1)
    bias[...] = jnp.where((seg == seg.T) & (key_id <= token_id), 0.0, -1e30)
    vT[128:144, :] = jnp.where(lax.broadcasted_iota(jnp.int32, (16, KEYS), 0) == 0, 1.0, 0.0).astype(bf16)
    prepare_keys(0, sk_v[...], sv_v[...])
    for part in range(PARTS):
        ready(0, part)

    def before_chunk(chunk):
        for slot, part in ARRIVALS[chunk]:
            if slot == 3:
                arrived(3, part)
                spread(3, 6, part, ahead)
                spread(3, 4, part, other)
            if slot == 2:
                arrived(2, part)
                spread(2, 5, part, other)
            if slot == 6:
                arrived(6, part)
                spread(6, 7, part, other)
        for slot, part in ARRIVALS[chunk]:
            if slot in (1, 4, 5, 7):
                arrived(slot, part)
            ready(slot, part)

    steps = [(chunk, head) for chunk in range(len(CHUNKS)) for head in range(HEADS)]
    peak, fade = {}, {}

    def score_strip(index, at, count):
        chunk, head = steps[index]
        start = CHUNKS[chunk][0] + at
        s = dot(k2[start:start + count, :], qT[:, head_cols(head)])
        if chunk == 0 and at < TOKENS:
            s = s + bias[at:at + count, :]
        s_buf[index % 2, at:at + count, :] = s
        part = jnp.max(s.reshape(count // 8, 8, TOKENS), 0)
        peak[index] = part if index not in peak else jnp.maximum(peak[index], part)

    def finish_peak(index):
        chunk, head = steps[index]
        cols = head_cols(head)
        highest = jnp.max(peak[index], 0, keepdims=True)
        if chunk > 0:
            before = top[:, cols]
            highest = jnp.maximum(highest, before)
            fade[index] = jnp.exp2(before - highest)
        top[:, cols] = highest
        tops[chunk:chunk + 1, cols] = highest
        peak[index] = highest

    def weight_strip(index, at, count):
        chunk, head = steps[index]
        start = CHUNKS[chunk][0] + at
        p_buf[start:start + count, head_cols(head)] = jnp.exp2(
            s_buf[index % 2, at:at + count, :] - peak[index]
        ).astype(bf16)

    def gather_values(index):
        chunk, head = steps[index]
        cols = head_cols(head)
        start, count = CHUNKS[chunk]
        found = dot(vT[:, start:start + count], p_buf[start:start + count, cols])
        if chunk > 0:
            total[:, cols] = total[:, cols] * fade[index] + found[128:129]
            acc[:, cols] = acc[:, cols] * fade[index] + found[:128]
        else:
            total[:, cols] = found[128:129]
            acc[:, cols] = found[:128]

    for at, count in strips(CHUNKS[0][1]):
        score_strip(0, at, count)
    for index in range(len(steps)):
        finish_peak(index)
        now = strips(CHUNKS[steps[index][0]][1])
        later = []
        if index + 1 < len(steps):
            chunk = steps[index + 1][0]
            if chunk != steps[index][0]:
                before_chunk(chunk)
            later = strips(CHUNKS[chunk][1])
        for turn in range(max(len(now), len(later))):
            if turn < len(later):
                score_strip(index + 1, *later[turn])
            if turn < len(now):
                weight_strip(index, *now[turn])
            if turn == 0 and index > 0:
                gather_values(index - 1)
    gather_values(len(steps) - 1)

    for head in range(HEADS):
        cols = head_cols(head)
        inverse = 1.0 / total[:, cols]
        out = acc[:, cols] * inverse
        delta[:, cols] = jnp.sum(out * dT[:, cols].astype(f32), 0, keepdims=True)
        out_v[:, head * 128:(head + 1) * 128] = out.T.astype(bf16)
        for chunk in range(len(CHUNKS)):
            factor[chunk:chunk + 1, cols] = jnp.exp2(tops[chunk:chunk + 1, cols] - top[:, cols]) * inverse

    store(out_v, out_ref)

    def back(start, count, chunk, values):
        for head in range(HEADS):
            cols = head_cols(head)
            weights = p_buf[start:start + count, cols] * factor[chunk:chunk + 1, cols].astype(bf16)
            p_buf[start:start + count, cols] = weights
            d_weights = dot(values, dT[:, cols])
            d_buf[start:start + count, cols] = weights * (d_weights - delta[:, cols]).astype(bf16)
        rows = slice(start, start + count)
        return dot(d_buf[rows, :], qs[...]) * SCALE, dot(p_buf[rows, :], ds[...])

    def back_part(slot, part):
        return back(START[slot, part], PART, CHUNK_OF[slot, part], kv[slot, part, 1])

    def for_other(index, part, slot):
        dk, dv = back_part(slot, part)
        sib_send[index, part, :, 0:128] = dk.astype(bf16)
        sib_send[index, part, :, 128:256] = dv.astype(bf16)

    def hold(index, part, slot):
        dk, dv = back_part(slot, part)
        keep[index, part, :, 0:128] = dk
        keep[index, part, :, 128:256] = dv

    def to_other(*places):
        for index, part in places:
            landing = LANDING[index]
            send(
                sib_send.at[index, part], sib_recv.at[landing, part], sib_s.at[index, part], sib_r.at[landing, part],
                {"ctx": other},
            )

    def landed(buffer, sems, index, part):
        pltpu.make_async_remote_copy(
            src_ref=buffer.at[index, part], dst_ref=buffer.at[index, part],
            send_sem=sems.at[index, part], recv_sem=sems.at[index, part],
            device_id={"ctx": other}, device_id_type=MESH,
        ).wait_recv()

    def to_chips(*places):
        for index, part in places:
            landed(sib_recv, sib_r, (0, 2, 1)[index], part)
            if index == 2:
                landed(x_recv, x_r, 0, part)
        for index, part in places:
            row = (0, 2, 1)[index]
            value = keep[row, part] + sib_recv[row, part].astype(f32)
            if index == 2:
                value = value + x_recv[0, part].astype(f32)
            x_send[index, part] = value.astype(bf16)
        for index, part in places:
            peer = behind if index == 1 else ahead
            send(x_send.at[index, part], x_recv.at[index, part], x_s.at[index, part], x_r.at[index, part], {"ctx": peer})

    def opposite(part):
        for_other(0, part, 7)
        hold(0, part, 6)

    def sides_other(part):
        for_other(1, part, 4)
        for_other(2, part, 5)

    def sides_same(part):
        hold(2, part, 3)
        hold(1, part, 2)

    def own(part):
        for_other(3, part, 1)
        hold(3, part, 0)

    def exchange(part):
        landed(sib_recv, sib_r, 3, part)
        landed(x_recv, x_r, 1, part)
        landed(x_recv, x_r, 2, part)
        mine = keep[3, part] + sib_recv[3, part].astype(f32)
        mine = mine + x_recv[1, part].astype(f32) + x_recv[2, part].astype(f32)
        keep[3, part] = mine
        for owner in range(8):
            y_send[part, owner] = mine[owner * 16:owner * 16 + 16, :].astype(bf16)
        for step in (4, 3, 5, 2, 6, 1, 7):
            peer = (dp + step) % 8
            send(y_send.at[part, peer], y_recv.at[part, step], y_s.at[part, step], y_r.at[part, step], {"dp": peer})

    def finish(part):
        for step in range(1, 8):
            landed(y_recv, y_r, part, step)
        mine = keep[3, part, pl.ds(pl.multiple_of(dp * 16, 16), 16), :]
        for step in range(1, 8):
            mine = mine + y_recv[part, step].astype(f32)
        dpk_v[part * 16:part * 16 + 16, :] = mine[:, 0:128]
        dpv_v[part * 16:part * 16 + 16, :] = mine[:, 128:256]

    def own_keys():
        dk, dv = back(0, TOKENS, 0, sv_v[...])
        dsk_v[...] = dk.astype(bf16)
        dsv_v[...] = dv.astype(bf16)

    def queries_gradient(head):
        turned = dot(kT[...], d_buf[:, head_cols(head)]) * SCALE
        dq_v[:, head * 128:(head + 1) * 128] = turned.T.astype(bf16)

    opposite(0)
    opposite(1)
    to_other((0, 0), (0, 1))
    opposite(2)
    sides_other(0)
    to_other((0, 2), (1, 0), (2, 0))
    to_chips((0, 0), (0, 1))
    sides_same(0)
    sides_other(1)
    to_other((1, 1), (2, 1))
    to_chips((0, 2), (1, 0))
    sides_same(1)
    sides_other(2)
    to_other((1, 2), (2, 2))
    to_chips((1, 1))
    sides_same(2)
    own(0)
    to_other((3, 0))
    to_chips((1, 2), (2, 0))
    own(1)
    own(2)
    to_other((3, 1), (3, 2))
    to_chips((2, 1), (2, 2))
    own_keys()
    for head in range(HEADS):
        queries_gradient(head)
    store(dsk_v, dsk_ref)
    store(dsv_v, dsv_ref)
    store(dq_v, dq_ref)
    for part in range(PARTS):
        exchange(part)
    for part in range(PARTS):
        finish(part)
    store(dpk_v, dpk_ref)
    store(dpv_v, dpv_ref)
    for copy in sends:
        copy.wait_send()
    for copy in stores:
        copy.wait()


def hand_over(*refs):
    sources, targets, held, (in_s, out_s) = refs[:6], refs[6:12], refs[12:18], refs[18:]
    loads = [pltpu.make_async_copy(sources[i], held[i], in_s.at[i]) for i in range(6)]
    stores = [pltpu.make_async_copy(held[i], targets[i], out_s.at[i]) for i in range(6)]
    for load in loads:
        load.start()
    for load, store in zip(loads, stores):
        load.wait()
        store.start()
    for store in stores:
        store.wait()


def shards(queries, suffix_keys, suffix_values, pre_keys, pre_values, segments, d_out):
    anywhere = pl.BlockSpec(memory_space=pl.ANY)
    dma = pltpu.SemaphoreType.DMA
    shapes = [
        ((TOKENS, HEADS * HEAD_WIDTH), bf16),
        ((TOKENS, HEADS * HEAD_WIDTH), bf16),
        ((TOKENS, HEAD_WIDTH), bf16),
        ((TOKENS, HEAD_WIDTH), bf16),
        ((PIECE, HEAD_WIDTH), f32),
        ((PIECE, HEAD_WIDTH), f32),
    ]
    out_shape = [jax.ShapeDtypeStruct(shape, dtype) for shape, dtype in shapes]
    results = pl.pallas_call(
        kernel,
        out_shape=out_shape,
        in_specs=[anywhere] * 7,
        out_specs=[anywhere] * 6,
        scratch_shapes=[
            pltpu.VMEM((TOKENS, HEADS * HEAD_WIDTH), bf16),
            pltpu.VMEM((TOKENS, HEAD_WIDTH), bf16),
            pltpu.VMEM((TOKENS, HEAD_WIDTH), bf16),
            pltpu.VMEM((OWN, HEAD_WIDTH), bf16),
            pltpu.VMEM((OWN, HEAD_WIDTH), bf16),
            pltpu.VMEM((1, TOKENS), jnp.int32),
            pltpu.VMEM((TOKENS, HEADS * HEAD_WIDTH), bf16),
        ] + [pltpu.VMEM(shape, dtype) for shape, dtype in shapes] + [
            pltpu.VMEM((8, PARTS, 2, PART, HEAD_WIDTH), bf16),
            pltpu.VMEM((256, ROWS), bf16),
            pltpu.VMEM((128, ROWS), bf16),
            pltpu.VMEM((ROWS, HEAD_WIDTH), bf16),
            pltpu.VMEM((ROWS, HEAD_WIDTH), bf16),
            pltpu.VMEM((128, KEYS), bf16),
            pltpu.VMEM((144, KEYS), bf16),
            pltpu.VMEM((KEYS, 256), bf16),
            pltpu.VMEM((TOKENS, TOKENS), f32),
            pltpu.VMEM((1, ROWS), f32),
            pltpu.VMEM((1, ROWS), f32),
            pltpu.VMEM((128, ROWS), f32),
            pltpu.VMEM((8, ROWS), f32),
            pltpu.VMEM((1, ROWS), f32),
            pltpu.VMEM((8, ROWS), f32),
            pltpu.VMEM((2, 768, TOKENS), f32),
            pltpu.VMEM((KEYS, ROWS), bf16),
            pltpu.VMEM((KEYS, ROWS), bf16),
            pltpu.VMEM((4, PARTS, PART, 256), f32),
            pltpu.VMEM((4, PARTS, PART, 256), bf16),
            pltpu.VMEM((4, PARTS, PART, 256), bf16),
            pltpu.VMEM((3, PARTS, PART, 256), bf16),
            pltpu.VMEM((3, PARTS, PART, 256), bf16),
            pltpu.VMEM((PARTS, 8, 16, 256), bf16),
            pltpu.VMEM((PARTS, 8, 16, 256), bf16),
            dma((7,)), dma((10,)), dma((21,)), dma((8, PARTS)), dma((4, PARTS)), dma((4, PARTS)),
            dma((3, PARTS)), dma((3, PARTS)), dma((PARTS, 8)), dma((PARTS, 8)),
        ],
        compiler_params=pltpu.CompilerParams(
            collective_id=0, has_side_effects=True, vmem_limit_bytes=60 << 20
        ),
    )(queries, suffix_keys, suffix_values, pre_keys, pre_values, segments, d_out)
    return pl.pallas_call(
        hand_over,
        out_shape=out_shape,
        in_specs=[anywhere] * 6,
        out_specs=[anywhere] * 6,
        scratch_shapes=[pltpu.VMEM(shape, dtype) for shape, dtype in shapes] + [dma((6,)), dma((6,))],
    )(*results)


def solution(mesh):
    split = P(("ctx", "dp"), "mp")
    in_specs = (split, split, split, P("ctx", "mp"), P("ctx", "mp"), P(("ctx", "dp"), None), split)
    return jax.shard_map(shards, mesh=mesh, in_specs=in_specs, out_specs=(split,) * 6, check_vma=False)
```

```python
import jax
import jax.numpy as jnp
from jax import lax
from jax.experimental import pallas as pl
from jax.experimental.pallas import tpu as pltpu
from jax.sharding import PartitionSpec as P

HEAD_WIDTH = 128
HEADS = 5
TOKENS = 256
ROWS = HEADS * TOKENS
OWN = 384
PIECE = 48
SCALE = HEAD_WIDTH ** (-0.5)
LOG2_SCALE = 1.4426950408889634 * SCALE
MESH = pl.DeviceIdType.MESH
bf16 = jnp.bfloat16
f32 = jnp.float32

PART = 128
PARTS = 3
ARRIVALS = [
    [(0, 0), (0, 1), (0, 2)],
    [(1, 0), (1, 1), (1, 2)],
    [(2, 1), (3, 1)],
    [(2, 2), (3, 2), (4, 1), (5, 1)],
    [(2, 0), (3, 0), (6, 0), (4, 2), (5, 2)],
    [(4, 0), (5, 0), (6, 1), (7, 0)],
    [(6, 2), (7, 1), (7, 2)],
]
KEYS = TOKENS + 8 * OWN
START, CHUNK_OF, CHUNKS = {}, {}, []
for chunk, arriving in enumerate(ARRIVALS):
    begin = 0 if chunk == 0 else sum(CHUNKS[-1])
    at = TOKENS if chunk == 0 else begin
    for place in arriving:
        START[place], CHUNK_OF[place] = at, chunk
        at += PART
    CHUNKS.append((begin, at - begin))
STRIP = 256
LANDING = {0: 0, 1: 2, 2: 1, 3: 3}


def dot(left, right):
    return lax.dot_general(left, right, (((1,), (0,)), ((), ())), preferred_element_type=f32)


def head_cols(head):
    return slice(head * TOKENS, (head + 1) * TOKENS)


def strips(count):
    return [(at, min(STRIP, count - at)) for at in range(0, count, STRIP)]


def kernel(
    q_ref, sk_ref, sv_ref, pk_ref, pv_ref, seg_ref, do_ref,
    out_ref, dq_ref, dsk_ref, dsv_ref, dpk_ref, dpv_ref,
    q_v, sk_v, sv_v, pk_v, pv_v, seg_v, do_v,
    kv, qT, dT, qs, ds, kT, vT, k2, bias, top, total, acc, tops, delta, factor, s_buf, p_buf, d_buf, vn, g_buf,
    keep, sib_send, sib_recv, x_send, x_recv, y_send, y_recv,
    in_s, ag_s, ag_r, sib_s, sib_r, x_s, x_r, y_s, y_r,
):
    ctx = lax.axis_index("ctx")
    dp = lax.axis_index("dp")
    core = ctx % 2
    chip = ctx // 2
    ahead = ((chip + 1 + 2 * core) % 4) * 2 + core
    behind = ((chip + 3 + 2 * core) % 4) * 2 + core
    opposite_chip = ((chip + 2) % 4) * 2 + core
    other = chip * 2 + (1 - core)

    barrier = pltpu.get_barrier_semaphore()
    for peer in (ahead, behind, opposite_chip, other):
        pl.semaphore_signal(barrier, inc=1, device_id={"ctx": peer}, device_id_type=MESH)
    for step in range(1, 8):
        pl.semaphore_signal(barrier, inc=1, device_id={"dp": (dp + step) % 8}, device_id_type=MESH)

    loads = {}
    for index, (name, source, target) in enumerate((
        ("pk", pk_ref, pk_v), ("pv", pv_ref, pv_v), ("q", q_ref, q_v), ("seg", seg_ref, seg_v),
        ("sk", sk_ref, sk_v), ("sv", sv_ref, sv_v), ("do", do_ref, do_v),
    )):
        loads[name] = pltpu.make_async_copy(source, target, in_s.at[index])
        loads[name].start()
    sends = []

    def send(src, dst, s_sem, r_sem, device):
        copy = pltpu.make_async_remote_copy(
            src_ref=src, dst_ref=dst, send_sem=s_sem, recv_sem=r_sem, device_id=device, device_id_type=MESH
        )
        copy.start()
        sends.append(copy)

    counter = []

    def spread(source, slot, part, peer):
        index = len(counter)
        counter.append(0)
        send(kv.at[source, part], kv.at[slot, part], ag_s.at[index], ag_r.at[slot, part], {"ctx": peer})

    def arrived(slot, part):
        pltpu.make_async_remote_copy(
            src_ref=kv.at[slot, part], dst_ref=kv.at[slot, part], send_sem=ag_s.at[0], recv_sem=ag_r.at[slot, part],
            device_id={"ctx": other}, device_id_type=MESH,
        ).wait_recv()

    def prepare_keys(start, keys, values):
        count = keys.shape[0]
        kT[:, start:start + count] = keys.T
        vT[0:128, start:start + count] = values.T
        vn[start:start + count, :] = values
        scaled = keys.astype(f32) * LOG2_SCALE
        high = scaled.astype(bf16)
        k2[start:start + count, 0:128] = high
        k2[start:start + count, 128:256] = (scaled - high.astype(f32)).astype(bf16)

    def ready(slot, part):
        prepare_keys(START[slot, part], kv[slot, part, 0], kv[slot, part, 1])

    loads["pk"].wait()
    loads["pv"].wait()
    for part in range(PARTS):
        for owner in range(8):
            rows = slice(owner * PIECE + part * 16, owner * PIECE + part * 16 + 16)
            kv[0, part, 0, owner * 16:owner * 16 + 16, :] = pk_v[rows, :]
            kv[0, part, 1, owner * 16:owner * 16 + 16, :] = pv_v[rows, :]
    pl.semaphore_wait(barrier, 11)
    for part in (1, 2, 0):
        if part == 0:
            spread(0, 6, part, opposite_chip)
        spread(0, 3, part, ahead)
        spread(0, 2, part, behind)
        spread(0, 1, part, other)

    loads["q"].wait()
    loads["seg"].wait()
    loads["sk"].wait()
    loads["sv"].wait()
    loads["do"].wait()
    for head in range(HEADS):
        cols = head_cols(head)
        width = slice(head * 128, (head + 1) * 128)
        q_head, do_head = q_v[:, width], do_v[:, width]
        q_turned = q_head.T
        qT[0:128, cols] = q_turned
        qT[128:256, cols] = q_turned
        dT[:, cols] = do_head.T
        qs[cols, :] = q_head
        ds[cols, :] = do_head
    seg = jnp.broadcast_to(seg_v[...].astype(f32), (TOKENS, TOKENS))
    key_id = lax.broadcasted_iota(jnp.int32, (TOKENS, TOKENS), 0)
    token_id = lax.broadcasted_iota(jnp.int32, (TOKENS, TOKENS), 1)
    bias[...] = jnp.where((seg == seg.T) & (key_id <= token_id), 0.0, -1e30)
    vT[128:144, :] = jnp.where(lax.broadcasted_iota(jnp.int32, (16, KEYS), 0) == 0, 1.0, 0.0).astype(bf16)
    prepare_keys(0, sk_v[...], sv_v[...])
    for part in range(PARTS):
        ready(0, part)

    def before_chunk(chunk):
        for slot, part in ARRIVALS[chunk]:
            if slot == 3:
                arrived(3, part)
                if part > 0:
                    spread(3, 6, part, ahead)
                spread(3, 4, part, other)
            if slot == 2:
                arrived(2, part)
                spread(2, 5, part, other)
            if slot == 6 and part == 0:
                arrived(6, part)
                spread(6, 7, part, other)
        for slot, part in ARRIVALS[chunk]:
            if slot in (1, 4, 5, 7):
                arrived(slot, part)
            ready(slot, part)

    steps = [(chunk, head) for chunk in range(len(CHUNKS)) for head in range(HEADS)]
    peak, fade = {}, {}

    def score_strip(index, at, count):
        chunk, head = steps[index]
        start = CHUNKS[chunk][0] + at
        s = dot(k2[start:start + count, :], qT[:, head_cols(head)])
        if chunk == 0 and at < TOKENS:
            s = s + bias[at:at + count, :]
        s_buf[index % 2, at:at + count, :] = s
        part = jnp.max(s.reshape(count // 8, 8, TOKENS), 0)
        peak[index] = part if index not in peak else jnp.maximum(peak[index], part)

    def finish_peak(index):
        chunk, head = steps[index]
        cols = head_cols(head)
        highest = jnp.max(peak[index], 0, keepdims=True)
        if chunk > 0:
            before = top[:, cols]
            highest = jnp.maximum(highest, before)
            fade[index] = jnp.exp2(before - highest)
        top[:, cols] = highest
        tops[chunk:chunk + 1, cols] = highest
        peak[index] = highest

    def weight_strip(index, at, count):
        chunk, head = steps[index]
        start = CHUNKS[chunk][0] + at
        p_buf[start:start + count, head_cols(head)] = jnp.exp2(
            s_buf[index % 2, at:at + count, :] - peak[index]
        ).astype(bf16)

    def gather_values(index):
        chunk, head = steps[index]
        cols = head_cols(head)
        start, count = CHUNKS[chunk]
        found = dot(vT[:, start:start + count], p_buf[start:start + count, cols])
        if chunk > 0:
            total[:, cols] = total[:, cols] * fade[index] + found[128:129]
            acc[:, cols] = acc[:, cols] * fade[index] + found[:128]
        else:
            total[:, cols] = found[128:129]
            acc[:, cols] = found[:128]

    def weight_gradients(index):
        chunk, head = steps[index]
        start, count = CHUNKS[chunk]
        g_buf[start:start + count, head_cols(head)] = dot(vn[start:start + count, :], dT[:, head_cols(head)])

    for at, count in strips(CHUNKS[0][1]):
        score_strip(0, at, count)
    for index in range(len(steps)):
        finish_peak(index)
        now = strips(CHUNKS[steps[index][0]][1])
        later = []
        if index + 1 < len(steps):
            chunk = steps[index + 1][0]
            if chunk != steps[index][0]:
                before_chunk(chunk)
            later = strips(CHUNKS[chunk][1])
        for turn in range(max(len(now), len(later))):
            if turn < len(later):
                score_strip(index + 1, *later[turn])
            if turn < len(now):
                weight_strip(index, *now[turn])
            if turn == 0 and index > 0:
                gather_values(index - 1)
        weight_gradients(index)
        if steps[index] in ((4, 1), (5, 1)):
            part = steps[index][0] - 3
            arrived(6, part)
            spread(6, 7, part, other)
    gather_values(len(steps) - 1)

    for head in range(HEADS):
        cols = head_cols(head)
        inverse = 1.0 / total[:, cols]
        out = acc[:, cols] * inverse
        delta[:, cols] = jnp.sum(out * dT[:, cols].astype(f32), 0, keepdims=True)
        acc[:, cols] = out
        for chunk in range(len(CHUNKS)):
            factor[chunk:chunk + 1, cols] = jnp.exp2(tops[chunk:chunk + 1, cols] - top[:, cols]) * inverse

    def back(start, count, chunk):
        for head in range(HEADS):
            cols = head_cols(head)
            weights = p_buf[start:start + count, cols] * factor[chunk:chunk + 1, cols].astype(bf16)
            p_buf[start:start + count, cols] = weights
            d_weights = g_buf[start:start + count, cols]
            d_buf[start:start + count, cols] = weights * (d_weights - delta[:, cols]).astype(bf16)
        rows = slice(start, start + count)
        return dot(d_buf[rows, :], qs[...]) * SCALE, dot(p_buf[rows, :], ds[...])

    def back_part(slot, part):
        return back(START[slot, part], PART, CHUNK_OF[slot, part])

    def for_other(index, part, slot):
        dk, dv = back_part(slot, part)
        sib_send[index, part, :, 0:128] = dk.astype(bf16)
        sib_send[index, part, :, 128:256] = dv.astype(bf16)

    def hold(index, part, slot):
        dk, dv = back_part(slot, part)
        keep[index, part, :, 0:128] = dk
        keep[index, part, :, 128:256] = dv

    def to_other(*places):
        for index, part in places:
            landing = LANDING[index]
            send(
                sib_send.at[index, part], sib_recv.at[landing, part], sib_s.at[index, part], sib_r.at[landing, part],
                {"ctx": other},
            )

    def landed(buffer, sems, index, part):
        pltpu.make_async_remote_copy(
            src_ref=buffer.at[index, part], dst_ref=buffer.at[index, part],
            send_sem=sems.at[index, part], recv_sem=sems.at[index, part],
            device_id={"ctx": other}, device_id_type=MESH,
        ).wait_recv()

    def to_chips(*places):
        for index, part in places:
            landed(sib_recv, sib_r, (0, 2, 1)[index], part)
            if index == 2:
                landed(x_recv, x_r, 0, part)
        for index, part in places:
            row = (0, 2, 1)[index]
            value = keep[row, part] + sib_recv[row, part].astype(f32)
            if index == 2:
                value = value + x_recv[0, part].astype(f32)
            x_send[index, part] = value.astype(bf16)
        for index, part in places:
            peer = behind if index == 1 else ahead
            send(x_send.at[index, part], x_recv.at[index, part], x_s.at[index, part], x_r.at[index, part], {"ctx": peer})

    def opposite(part):
        for_other(0, part, 7)
        hold(0, part, 6)

    def sides_other(part):
        for_other(1, part, 4)
        for_other(2, part, 5)

    def sides_same(part):
        hold(2, part, 3)
        hold(1, part, 2)

    def own(part):
        for_other(3, part, 1)
        hold(3, part, 0)

    def exchange(part):
        landed(sib_recv, sib_r, 3, part)
        landed(x_recv, x_r, 1, part)
        landed(x_recv, x_r, 2, part)
        mine = keep[3, part] + sib_recv[3, part].astype(f32)
        mine = mine + x_recv[1, part].astype(f32) + x_recv[2, part].astype(f32)
        keep[3, part] = mine
        for owner in range(8):
            y_send[part, owner] = mine[owner * 16:owner * 16 + 16, :].astype(bf16)
        for step in (4, 3, 5, 2, 6, 1, 7):
            peer = (dp + step) % 8
            send(y_send.at[part, peer], y_recv.at[part, step], y_s.at[part, step], y_r.at[part, step], {"dp": peer})

    def finish(part):
        for step in range(1, 8):
            landed(y_recv, y_r, part, step)
        mine = keep[3, part, pl.ds(pl.multiple_of(dp * 16, 16), 16), :]
        for step in range(1, 8):
            mine = mine + y_recv[part, step].astype(f32)
        dpk_ref[part * 16:part * 16 + 16, :] = mine[:, 0:128]
        dpv_ref[part * 16:part * 16 + 16, :] = mine[:, 128:256]

    def own_keys():
        dk, dv = back(0, TOKENS, 0)
        dsk_ref[...] = dk.astype(bf16)
        dsv_ref[...] = dv.astype(bf16)

    def attended(head):
        out_ref[:, head * 128:(head + 1) * 128] = acc[:, head_cols(head)].T.astype(bf16)

    def queries_gradient(head):
        turned = dot(kT[...], d_buf[:, head_cols(head)]) * SCALE
        dq_ref[:, head * 128:(head + 1) * 128] = turned.T.astype(bf16)

    opposite(0)
    opposite(1)
    to_other((0, 0), (0, 1))
    opposite(2)
    sides_other(0)
    to_other((0, 2), (1, 0), (2, 0))
    to_chips((0, 0), (0, 1))
    sides_same(0)
    sides_other(1)
    to_other((1, 1), (2, 1))
    to_chips((0, 2), (1, 0))
    sides_same(1)
    sides_other(2)
    to_other((1, 2), (2, 2))
    to_chips((1, 1))
    sides_same(2)
    own(0)
    to_other((3, 0))
    to_chips((1, 2), (2, 0))
    own(1)
    own(2)
    to_other((3, 1), (3, 2))
    to_chips((2, 1), (2, 2))
    own_keys()
    for head in range(HEADS):
        attended(head)
        queries_gradient(head)
    for part in range(PARTS):
        exchange(part)
    for part in range(PARTS):
        finish(part)
    for copy in sends:
        copy.wait_send()


def hand_over(*refs):
    copies = [pltpu.make_async_copy(refs[i], refs[6 + i], refs[12].at[i]) for i in range(6)]
    for copy in copies:
        copy.start()
    for copy in copies:
        copy.wait()


def shards(queries, suffix_keys, suffix_values, pre_keys, pre_values, segments, d_out):
    anywhere = pl.BlockSpec(memory_space=pl.ANY)
    inside = pl.BlockSpec(memory_space=pltpu.VMEM)
    dma = pltpu.SemaphoreType.DMA
    shapes = [
        ((TOKENS, HEADS * HEAD_WIDTH), bf16),
        ((TOKENS, HEADS * HEAD_WIDTH), bf16),
        ((TOKENS, HEAD_WIDTH), bf16),
        ((TOKENS, HEAD_WIDTH), bf16),
        ((PIECE, HEAD_WIDTH), f32),
        ((PIECE, HEAD_WIDTH), f32),
    ]
    out_shape = [jax.ShapeDtypeStruct(shape, dtype) for shape, dtype in shapes]
    results = pl.pallas_call(
        kernel,
        out_shape=[pltpu.VMEM(shape, dtype) for shape, dtype in shapes],
        in_specs=[anywhere] * 7,
        out_specs=[inside] * 6,
        scratch_shapes=[
            pltpu.VMEM((TOKENS, HEADS * HEAD_WIDTH), bf16),
            pltpu.VMEM((TOKENS, HEAD_WIDTH), bf16),
            pltpu.VMEM((TOKENS, HEAD_WIDTH), bf16),
            pltpu.VMEM((OWN, HEAD_WIDTH), bf16),
            pltpu.VMEM((OWN, HEAD_WIDTH), bf16),
            pltpu.VMEM((1, TOKENS), jnp.int32),
            pltpu.VMEM((TOKENS, HEADS * HEAD_WIDTH), bf16),
            pltpu.VMEM((8, PARTS, 2, PART, HEAD_WIDTH), bf16),
            pltpu.VMEM((256, ROWS), bf16),
            pltpu.VMEM((128, ROWS), bf16),
            pltpu.VMEM((ROWS, HEAD_WIDTH), bf16),
            pltpu.VMEM((ROWS, HEAD_WIDTH), bf16),
            pltpu.VMEM((128, KEYS), bf16),
            pltpu.VMEM((144, KEYS), bf16),
            pltpu.VMEM((KEYS, 256), bf16),
            pltpu.VMEM((TOKENS, TOKENS), f32),
            pltpu.VMEM((1, ROWS), f32),
            pltpu.VMEM((1, ROWS), f32),
            pltpu.VMEM((128, ROWS), f32),
            pltpu.VMEM((8, ROWS), f32),
            pltpu.VMEM((1, ROWS), f32),
            pltpu.VMEM((8, ROWS), f32),
            pltpu.VMEM((2, 768, TOKENS), f32),
            pltpu.VMEM((KEYS, ROWS), bf16),
            pltpu.VMEM((KEYS, ROWS), bf16),
            pltpu.VMEM((KEYS, HEAD_WIDTH), bf16),
            pltpu.VMEM((KEYS, ROWS), f32),
            pltpu.VMEM((4, PARTS, PART, 256), f32),
            pltpu.VMEM((4, PARTS, PART, 256), bf16),
            pltpu.VMEM((4, PARTS, PART, 256), bf16),
            pltpu.VMEM((3, PARTS, PART, 256), bf16),
            pltpu.VMEM((3, PARTS, PART, 256), bf16),
            pltpu.VMEM((PARTS, 8, 16, 256), bf16),
            pltpu.VMEM((PARTS, 8, 16, 256), bf16),
            dma((7,)), dma((21,)), dma((8, PARTS)), dma((4, PARTS)), dma((4, PARTS)),
            dma((3, PARTS)), dma((3, PARTS)), dma((PARTS, 8)), dma((PARTS, 8)),
        ],
        compiler_params=pltpu.CompilerParams(
            collective_id=0, has_side_effects=True, vmem_limit_bytes=56 << 20
        ),
    )(queries, suffix_keys, suffix_values, pre_keys, pre_values, segments, d_out)
    return pl.pallas_call(
        hand_over,
        out_shape=out_shape,
        in_specs=[inside] * 6,
        out_specs=[anywhere] * 6,
        scratch_shapes=[dma((6,))],
        compiler_params=pltpu.CompilerParams(vmem_limit_bytes=2 << 20),
    )(*results)


def solution(mesh):
    split = P(("ctx", "dp"), "mp")
    in_specs = (split, split, split, P("ctx", "mp"), P("ctx", "mp"), P(("ctx", "dp"), None), split)
    return jax.shard_map(shards, mesh=mesh, in_specs=in_specs, out_specs=(split,) * 6, check_vma=False)
```

```python
import jax
import jax.numpy as jnp
from jax import lax
from jax.experimental import pallas as pl
from jax.experimental.pallas import tpu as pltpu
from jax.sharding import PartitionSpec as P

HEAD_WIDTH = 128
HEADS = 5
TOKENS = 256
ROWS = HEADS * TOKENS
OWN = 384
PIECE = 48
SCALE = HEAD_WIDTH ** (-0.5)
LOG2_SCALE = 1.4426950408889634 * SCALE
MESH = pl.DeviceIdType.MESH
bf16 = jnp.bfloat16
f32 = jnp.float32

PART = 128
PARTS = 3
ARRIVALS = [
    [(0, 0), (0, 1), (0, 2)],
    [(1, 0), (1, 1), (1, 2)],
    [(2, 1), (3, 1)],
    [(2, 2), (3, 2), (4, 1), (5, 1)],
    [(2, 0), (3, 0), (6, 0), (4, 2), (5, 2)],
    [(4, 0), (5, 0), (6, 1), (7, 0), (7, 1)],
    [(6, 2), (7, 2)],
]
KEYS = TOKENS + 8 * OWN
START, CHUNK_OF, CHUNKS = {}, {}, []
for chunk, arriving in enumerate(ARRIVALS):
    begin = 0 if chunk == 0 else sum(CHUNKS[-1])
    at = TOKENS if chunk == 0 else begin
    for place in arriving:
        START[place], CHUNK_OF[place] = at, chunk
        at += PART
    CHUNKS.append((begin, at - begin))
STRIP = 256
LANDING = {0: 0, 1: 2, 2: 1, 3: 3}
ROW_SENT = (0, 2, 1, 0)
RING = (1,)


def dot(left, right):
    return lax.dot_general(left, right, (((1,), (0,)), ((), ())), preferred_element_type=f32)


def head_cols(head):
    return slice(head * TOKENS, (head + 1) * TOKENS)


def strips(count):
    return [(at, min(STRIP, count - at)) for at in range(0, count, STRIP)]


def kernel(
    q_ref, sk_ref, sv_ref, pk_ref, pv_ref, seg_ref, do_ref,
    out_ref, dq_ref, dsk_ref, dsv_ref, dpk_ref, dpv_ref,
    q_v, sk_v, sv_v, pk_v, pv_v, seg_v, do_v,
    kv, qT, dT, qs, ds, kT, vT, k2, bias, top, total, acc, tops, delta, factor, s_buf, p_buf, d_buf, vn, g_buf,
    keep, sib_send, sib_recv, x_send, x_recv, y_send, y_recv,
    in_s, ag_s, ag_r, sib_s, sib_r, x_s, x_r, y_s, y_r,
):
    ctx = lax.axis_index("ctx")
    dp = lax.axis_index("dp")
    core = ctx % 2
    chip = ctx // 2
    ahead = ((chip + 1 + 2 * core) % 4) * 2 + core
    behind = ((chip + 3 + 2 * core) % 4) * 2 + core
    opposite_chip = ((chip + 2) % 4) * 2 + core
    ahead_other = ((chip + 1 + 2 * core) % 4) * 2 + (1 - core)
    behind_other = ((chip + 3 + 2 * core) % 4) * 2 + (1 - core)
    other = chip * 2 + (1 - core)

    barrier = pltpu.get_barrier_semaphore()
    for peer in (ahead, behind, ahead_other, behind_other, opposite_chip, other):
        pl.semaphore_signal(barrier, inc=1, device_id={"ctx": peer}, device_id_type=MESH)
    for step in range(1, 8):
        pl.semaphore_signal(barrier, inc=1, device_id={"dp": (dp + step) % 8}, device_id_type=MESH)

    loads = {}
    for index, (name, source, target) in enumerate((
        ("pk", pk_ref, pk_v), ("pv", pv_ref, pv_v), ("q", q_ref, q_v), ("seg", seg_ref, seg_v),
        ("sk", sk_ref, sk_v), ("sv", sv_ref, sv_v), ("do", do_ref, do_v),
    )):
        loads[name] = pltpu.make_async_copy(source, target, in_s.at[index])
        loads[name].start()
    sends = []

    def send(src, dst, s_sem, r_sem, device):
        copy = pltpu.make_async_remote_copy(
            src_ref=src, dst_ref=dst, send_sem=s_sem, recv_sem=r_sem, device_id=device, device_id_type=MESH
        )
        copy.start()
        sends.append(copy)

    counter = []

    def spread(source, slot, part, peer):
        index = len(counter)
        counter.append(0)
        send(kv.at[source, part], kv.at[slot, part], ag_s.at[index], ag_r.at[slot, part], {"ctx": peer})

    def arrived(slot, part):
        pltpu.make_async_remote_copy(
            src_ref=kv.at[slot, part], dst_ref=kv.at[slot, part], send_sem=ag_s.at[0], recv_sem=ag_r.at[slot, part],
            device_id={"ctx": other}, device_id_type=MESH,
        ).wait_recv()

    def prepare_keys(start, keys, values):
        count = keys.shape[0]
        kT[:, start:start + count] = keys.T
        vT[0:128, start:start + count] = values.T
        vn[start:start + count, :] = values
        scaled = keys.astype(f32) * LOG2_SCALE
        high = scaled.astype(bf16)
        k2[start:start + count, 0:128] = high
        k2[start:start + count, 128:256] = (scaled - high.astype(f32)).astype(bf16)

    def ready(slot, part):
        prepare_keys(START[slot, part], kv[slot, part, 0], kv[slot, part, 1])

    loads["pk"].wait()
    loads["pv"].wait()
    for part in range(PARTS):
        for owner in range(8):
            rows = slice(owner * PIECE + part * 16, owner * PIECE + part * 16 + 16)
            kv[0, part, 0, owner * 16:owner * 16 + 16, :] = pk_v[rows, :]
            kv[0, part, 1, owner * 16:owner * 16 + 16, :] = pv_v[rows, :]
    pl.semaphore_wait(barrier, 13)
    for part in (1, 2, 0):
        if part == 0:
            spread(0, 6, part, opposite_chip)
        spread(0, 3, part, ahead)
        spread(0, 2, part, behind)
        spread(0, 1, part, other)

    loads["q"].wait()
    loads["seg"].wait()
    loads["sk"].wait()
    loads["sv"].wait()
    loads["do"].wait()
    for head in range(HEADS):
        cols = head_cols(head)
        width = slice(head * 128, (head + 1) * 128)
        q_head, do_head = q_v[:, width], do_v[:, width]
        q_turned = q_head.T
        qT[0:128, cols] = q_turned
        qT[128:256, cols] = q_turned
        dT[:, cols] = do_head.T
        qs[cols, :] = q_head
        ds[cols, :] = do_head
    seg = jnp.broadcast_to(seg_v[...].astype(f32), (TOKENS, TOKENS))
    key_id = lax.broadcasted_iota(jnp.int32, (TOKENS, TOKENS), 0)
    token_id = lax.broadcasted_iota(jnp.int32, (TOKENS, TOKENS), 1)
    bias[...] = jnp.where((seg == seg.T) & (key_id <= token_id), 0.0, -1e30)
    vT[128:144, :] = jnp.where(lax.broadcasted_iota(jnp.int32, (16, KEYS), 0) == 0, 1.0, 0.0).astype(bf16)
    prepare_keys(0, sk_v[...], sv_v[...])
    for part in range(PARTS):
        ready(0, part)

    def before_chunk(chunk):
        for slot, part in ARRIVALS[chunk]:
            if slot == 3:
                arrived(3, part)
                if part > 0:
                    spread(3, 6, part, ahead)
                if part == 2:
                    spread(3, 7, part, ahead_other)
                spread(3, 4, part, other)
            if slot == 2:
                arrived(2, part)
                spread(2, 5, part, other)
            if slot == 6 and part == 0:
                arrived(6, part)
                spread(6, 7, part, other)
        for slot, part in ARRIVALS[chunk]:
            if slot in (1, 4, 5, 7) or (slot, part) == (6, 2):
                arrived(slot, part)
            ready(slot, part)

    steps = [(chunk, head) for chunk in range(len(CHUNKS)) for head in range(HEADS)]
    peak, fade = {}, {}

    def score_strip(index, at, count):
        chunk, head = steps[index]
        start = CHUNKS[chunk][0] + at
        s = dot(k2[start:start + count, :], qT[:, head_cols(head)])
        if chunk == 0 and at < TOKENS:
            s = s + bias[at:at + count, :]
        s_buf[index % 2, at:at + count, :] = s
        part = jnp.max(s.reshape(count // 8, 8, TOKENS), 0)
        peak[index] = part if index not in peak else jnp.maximum(peak[index], part)

    def finish_peak(index):
        chunk, head = steps[index]
        cols = head_cols(head)
        highest = jnp.max(peak[index], 0, keepdims=True)
        if chunk > 0:
            before = top[:, cols]
            highest = jnp.maximum(highest, before)
            fade[index] = jnp.exp2(before - highest)
        top[:, cols] = highest
        tops[chunk:chunk + 1, cols] = highest
        peak[index] = highest

    def weight_strip(index, at, count):
        chunk, head = steps[index]
        start = CHUNKS[chunk][0] + at
        p_buf[start:start + count, head_cols(head)] = jnp.exp2(
            s_buf[index % 2, at:at + count, :] - peak[index]
        ).astype(bf16)

    def gather_values(index):
        chunk, head = steps[index]
        cols = head_cols(head)
        start, count = CHUNKS[chunk]
        found = dot(vT[:, start:start + count], p_buf[start:start + count, cols])
        if chunk > 0:
            total[:, cols] = total[:, cols] * fade[index] + found[128:129]
            acc[:, cols] = acc[:, cols] * fade[index] + found[:128]
        else:
            total[:, cols] = found[128:129]
            acc[:, cols] = found[:128]

    def weight_gradients(index):
        chunk, head = steps[index]
        start, count = CHUNKS[chunk]
        g_buf[start:start + count, head_cols(head)] = dot(vn[start:start + count, :], dT[:, head_cols(head)])

    for at, count in strips(CHUNKS[0][1]):
        score_strip(0, at, count)
    for index in range(len(steps)):
        finish_peak(index)
        now = strips(CHUNKS[steps[index][0]][1])
        later = []
        if index + 1 < len(steps):
            chunk = steps[index + 1][0]
            if chunk != steps[index][0]:
                before_chunk(chunk)
            later = strips(CHUNKS[chunk][1])
        for turn in range(max(len(now), len(later))):
            if turn < len(later):
                score_strip(index + 1, *later[turn])
            if turn < len(now):
                weight_strip(index, *now[turn])
            if turn == 0 and index > 0:
                gather_values(index - 1)
        weight_gradients(index)
        if steps[index] == (4, 1):
            arrived(6, 1)
            spread(6, 7, 1, other)
    gather_values(len(steps) - 1)

    for head in range(HEADS):
        cols = head_cols(head)
        inverse = 1.0 / total[:, cols]
        out = acc[:, cols] * inverse
        delta[:, cols] = jnp.sum(out * dT[:, cols].astype(f32), 0, keepdims=True)
        acc[:, cols] = out
        for chunk in range(len(CHUNKS)):
            factor[chunk:chunk + 1, cols] = jnp.exp2(tops[chunk:chunk + 1, cols] - top[:, cols]) * inverse

    def back(start, count, chunk):
        for head in range(HEADS):
            cols = head_cols(head)
            weights = p_buf[start:start + count, cols] * factor[chunk:chunk + 1, cols].astype(bf16)
            p_buf[start:start + count, cols] = weights
            d_weights = g_buf[start:start + count, cols]
            d_buf[start:start + count, cols] = weights * (d_weights - delta[:, cols]).astype(bf16)
        rows = slice(start, start + count)
        return dot(d_buf[rows, :], qs[...]) * SCALE, dot(p_buf[rows, :], ds[...])

    def back_part(slot, part):
        return back(START[slot, part], PART, CHUNK_OF[slot, part])

    def for_other(index, part, slot):
        dk, dv = back_part(slot, part)
        sib_send[index, part, :, 0:128] = dk.astype(bf16)
        sib_send[index, part, :, 128:256] = dv.astype(bf16)

    def hold(index, part, slot):
        dk, dv = back_part(slot, part)
        keep[index, part, :, 0:128] = dk
        keep[index, part, :, 128:256] = dv

    def to_other(*places):
        for index, part in places:
            landing = LANDING[index]
            send(
                sib_send.at[index, part], sib_recv.at[landing, part], sib_s.at[index, part], sib_r.at[landing, part],
                {"ctx": other},
            )

    def landed(buffer, sems, index, part):
        pltpu.make_async_remote_copy(
            src_ref=buffer.at[index, part], dst_ref=buffer.at[index, part],
            send_sem=sems.at[index, part], recv_sem=sems.at[index, part],
            device_id={"ctx": other}, device_id_type=MESH,
        ).wait_recv()

    def to_chips(*places):
        for index, part in places:
            landed(sib_recv, sib_r, ROW_SENT[index], part)
            if index == 2 and part in RING:
                landed(x_recv, x_r, 0, part)
        for index, part in places:
            row = ROW_SENT[index]
            value = keep[row, part] + sib_recv[row, part].astype(f32)
            if index == 2 and part in RING:
                value = value + x_recv[0, part].astype(f32)
            x_send[index, part] = value.astype(bf16)
        for index, part in places:
            peer = (ahead, behind, ahead, opposite_chip)[index]
            send(x_send.at[index, part], x_recv.at[index, part], x_s.at[index, part], x_r.at[index, part], {"ctx": peer})

    def opposite(part):
        for_other(0, part, 7)
        hold(0, part, 6)

    def sides_other(part):
        for_other(1, part, 4)
        for_other(2, part, 5)

    def sides_same(part):
        hold(2, part, 3)
        hold(1, part, 2)

    def own(part):
        for_other(3, part, 1)
        hold(3, part, 0)

    def exchange(part):
        landed(sib_recv, sib_r, 3, part)
        landed(x_recv, x_r, 1, part)
        landed(x_recv, x_r, 2, part)
        mine = keep[3, part] + sib_recv[3, part].astype(f32)
        mine = mine + x_recv[1, part].astype(f32) + x_recv[2, part].astype(f32)
        if part not in RING:
            landed(x_recv, x_r, 3, part)
            mine = mine + x_recv[3, part].astype(f32)
        keep[3, part] = mine
        for owner in range(8):
            y_send[part, owner] = mine[owner * 16:owner * 16 + 16, :].astype(bf16)
        for step in (4, 3, 5, 2, 6, 1, 7):
            peer = (dp + step) % 8
            send(y_send.at[part, peer], y_recv.at[part, step], y_s.at[part, step], y_r.at[part, step], {"dp": peer})

    def finish(part):
        for step in range(1, 8):
            landed(y_recv, y_r, part, step)
        mine = keep[3, part, pl.ds(pl.multiple_of(dp * 16, 16), 16), :]
        for step in range(1, 8):
            mine = mine + y_recv[part, step].astype(f32)
        dpk_ref[part * 16:part * 16 + 16, :] = mine[:, 0:128]
        dpv_ref[part * 16:part * 16 + 16, :] = mine[:, 128:256]

    def own_keys():
        dk, dv = back(0, TOKENS, 0)
        dsk_ref[...] = dk.astype(bf16)
        dsv_ref[...] = dv.astype(bf16)

    def attended(head):
        out_ref[:, head * 128:(head + 1) * 128] = acc[:, head_cols(head)].T.astype(bf16)

    def queries_gradient(head):
        turned = dot(kT[...], d_buf[:, head_cols(head)]) * SCALE
        dq_ref[:, head * 128:(head + 1) * 128] = turned.T.astype(bf16)

    opposite(0)
    to_other((0, 0))
    opposite(1)
    opposite(2)
    to_other((0, 1), (0, 2))
    to_chips((3, 0))
    sides_other(0)
    sides_same(0)
    to_other((1, 0), (2, 0))
    to_chips((0, 1), (3, 2))
    sides_other(1)
    sides_same(1)
    to_other((1, 1), (2, 1))
    to_chips((1, 0), (2, 0))
    sides_other(2)
    sides_same(2)
    to_other((1, 2), (2, 2))
    to_chips((1, 1))
    own(0)
    own(1)
    to_other((3, 0), (3, 1))
    to_chips((1, 2), (2, 2))
    to_chips((2, 1))
    own(2)
    own_keys()
    to_other((3, 2))
    for head in range(2):
        queries_gradient(head)
    exchange(0)
    for head in range(2, HEADS):
        queries_gradient(head)
    for head in range(HEADS):
        attended(head)
    exchange(1)
    exchange(2)
    for copy in sends:
        copy.wait_send()
    for part in range(PARTS):
        finish(part)


def hand_over(*refs):
    copies = [pltpu.make_async_copy(refs[i], refs[6 + i], refs[12].at[i]) for i in range(6)]
    for copy in copies:
        copy.start()
    for copy in copies:
        copy.wait()


def shards(queries, suffix_keys, suffix_values, pre_keys, pre_values, segments, d_out):
    anywhere = pl.BlockSpec(memory_space=pl.ANY)
    inside = pl.BlockSpec(memory_space=pltpu.VMEM)
    dma = pltpu.SemaphoreType.DMA
    shapes = [
        ((TOKENS, HEADS * HEAD_WIDTH), bf16),
        ((TOKENS, HEADS * HEAD_WIDTH), bf16),
        ((TOKENS, HEAD_WIDTH), bf16),
        ((TOKENS, HEAD_WIDTH), bf16),
        ((PIECE, HEAD_WIDTH), f32),
        ((PIECE, HEAD_WIDTH), f32),
    ]
    out_shape = [jax.ShapeDtypeStruct(shape, dtype) for shape, dtype in shapes]
    results = pl.pallas_call(
        kernel,
        out_shape=[pltpu.VMEM(shape, dtype) for shape, dtype in shapes],
        in_specs=[anywhere] * 7,
        out_specs=[inside] * 6,
        scratch_shapes=[
            pltpu.VMEM((TOKENS, HEADS * HEAD_WIDTH), bf16),
            pltpu.VMEM((TOKENS, HEAD_WIDTH), bf16),
            pltpu.VMEM((TOKENS, HEAD_WIDTH), bf16),
            pltpu.VMEM((OWN, HEAD_WIDTH), bf16),
            pltpu.VMEM((OWN, HEAD_WIDTH), bf16),
            pltpu.VMEM((1, TOKENS), jnp.int32),
            pltpu.VMEM((TOKENS, HEADS * HEAD_WIDTH), bf16),
            pltpu.VMEM((8, PARTS, 2, PART, HEAD_WIDTH), bf16),
            pltpu.VMEM((256, ROWS), bf16),
            pltpu.VMEM((128, ROWS), bf16),
            pltpu.VMEM((ROWS, HEAD_WIDTH), bf16),
            pltpu.VMEM((ROWS, HEAD_WIDTH), bf16),
            pltpu.VMEM((128, KEYS), bf16),
            pltpu.VMEM((144, KEYS), bf16),
            pltpu.VMEM((KEYS, 256), bf16),
            pltpu.VMEM((TOKENS, TOKENS), f32),
            pltpu.VMEM((1, ROWS), f32),
            pltpu.VMEM((1, ROWS), f32),
            pltpu.VMEM((128, ROWS), f32),
            pltpu.VMEM((8, ROWS), f32),
            pltpu.VMEM((1, ROWS), f32),
            pltpu.VMEM((8, ROWS), f32),
            pltpu.VMEM((2, 768, TOKENS), f32),
            pltpu.VMEM((KEYS, ROWS), bf16),
            pltpu.VMEM((KEYS, ROWS), bf16),
            pltpu.VMEM((KEYS, HEAD_WIDTH), bf16),
            pltpu.VMEM((KEYS, ROWS), f32),
            pltpu.VMEM((4, PARTS, PART, 256), f32),
            pltpu.VMEM((4, PARTS, PART, 256), bf16),
            pltpu.VMEM((4, PARTS, PART, 256), bf16),
            pltpu.VMEM((4, PARTS, PART, 256), bf16),
            pltpu.VMEM((4, PARTS, PART, 256), bf16),
            pltpu.VMEM((PARTS, 8, 16, 256), bf16),
            pltpu.VMEM((PARTS, 8, 16, 256), bf16),
            dma((7,)), dma((21,)), dma((8, PARTS)), dma((4, PARTS)), dma((4, PARTS)),
            dma((4, PARTS)), dma((4, PARTS)), dma((PARTS, 8)), dma((PARTS, 8)),
        ],
        compiler_params=pltpu.CompilerParams(
            collective_id=0, has_side_effects=True, vmem_limit_bytes=56 << 20
        ),
    )(queries, suffix_keys, suffix_values, pre_keys, pre_values, segments, d_out)
    return pl.pallas_call(
        hand_over,
        out_shape=out_shape,
        in_specs=[inside] * 6,
        out_specs=[anywhere] * 6,
        scratch_shapes=[dma((6,))],
        compiler_params=pltpu.CompilerParams(vmem_limit_bytes=2 << 20),
    )(*results)


def solution(mesh):
    split = P(("ctx", "dp"), "mp")
    in_specs = (split, split, split, P("ctx", "mp"), P("ctx", "mp"), P(("ctx", "dp"), None), split)
    return jax.shard_map(shards, mesh=mesh, in_specs=in_specs, out_specs=(split,) * 6, check_vma=False)
```

```python
import jax
import jax.numpy as jnp
from jax import lax
from jax.experimental import pallas as pl
from jax.experimental.pallas import tpu as pltpu
from jax.sharding import PartitionSpec as P

HEAD_WIDTH = 128
HEADS = 5
TOKENS = 256
ROWS = HEADS * TOKENS
OWN = 384
PIECE = 48
SCALE = HEAD_WIDTH ** (-0.5)
LOG2_SCALE = 1.4426950408889634 * SCALE
MESH = pl.DeviceIdType.MESH
bf16 = jnp.bfloat16
f32 = jnp.float32

PART = 128
PARTS = 3
ARRIVALS = [
    [(0, 0), (0, 1), (0, 2)],
    [(1, 0), (1, 1), (1, 2)],
    [(2, 1), (3, 1)],
    [(2, 2), (3, 2), (4, 1), (5, 1)],
    [(2, 0), (3, 0), (6, 0), (4, 2), (5, 2)],
    [(4, 0), (5, 0), (6, 1), (7, 0), (7, 1)],
    [(6, 2), (7, 2)],
]
KEYS = TOKENS + 8 * OWN
START, CHUNK_OF, CHUNKS = {}, {}, []
for chunk, arriving in enumerate(ARRIVALS):
    begin = 0 if chunk == 0 else sum(CHUNKS[-1])
    at = TOKENS if chunk == 0 else begin
    for place in arriving:
        START[place], CHUNK_OF[place] = at, chunk
        at += PART
    CHUNKS.append((begin, at - begin))
STRIP = 256
LANDING = {0: 0, 1: 2, 2: 1, 3: 3}
ROW_SENT = (0, 2, 1, 0)
RING = ()


def dot(left, right):
    return lax.dot_general(left, right, (((1,), (0,)), ((), ())), preferred_element_type=f32)


def head_cols(head):
    return slice(head * TOKENS, (head + 1) * TOKENS)


def strips(count):
    return [(at, min(STRIP, count - at)) for at in range(0, count, STRIP)]


def kernel(
    q_ref, sk_ref, sv_ref, pk_ref, pv_ref, seg_ref, do_ref,
    out_ref, dq_ref, dsk_ref, dsv_ref, dpk_ref, dpv_ref,
    q_v, sk_v, sv_v, pk_v, pv_v, seg_v, do_v,
    kv, qT, dT, qs, ds, kT, vT, k2, bias, top, total, acc, tops, delta, factor, s_buf, p_buf, d_buf, vn, g_buf,
    keep, sib_send, sib_recv, x_send, x_recv, y_send, y_recv,
    in_s, ag_s, ag_r, sib_s, sib_r, x_s, x_r, y_s, y_r,
):
    ctx = lax.axis_index("ctx")
    dp = lax.axis_index("dp")
    core = ctx % 2
    chip = ctx // 2
    ahead = ((chip + 1 + 2 * core) % 4) * 2 + core
    behind = ((chip + 3 + 2 * core) % 4) * 2 + core
    opposite_chip = ((chip + 2) % 4) * 2 + core
    ahead_other = ((chip + 1 + 2 * core) % 4) * 2 + (1 - core)
    behind_other = ((chip + 3 + 2 * core) % 4) * 2 + (1 - core)
    other = chip * 2 + (1 - core)

    barrier = pltpu.get_barrier_semaphore()
    for peer in (ahead, behind, ahead_other, behind_other, opposite_chip, other):
        pl.semaphore_signal(barrier, inc=1, device_id={"ctx": peer}, device_id_type=MESH)
    for step in range(1, 8):
        pl.semaphore_signal(barrier, inc=1, device_id={"dp": (dp + step) % 8}, device_id_type=MESH)

    loads = {}
    for index, (name, source, target) in enumerate((
        ("pk", pk_ref, pk_v), ("pv", pv_ref, pv_v), ("q", q_ref, q_v), ("seg", seg_ref, seg_v),
        ("sk", sk_ref, sk_v), ("sv", sv_ref, sv_v), ("do", do_ref, do_v),
    )):
        loads[name] = pltpu.make_async_copy(source, target, in_s.at[index])
        loads[name].start()
    sends = []

    def send(src, dst, s_sem, r_sem, device):
        copy = pltpu.make_async_remote_copy(
            src_ref=src, dst_ref=dst, send_sem=s_sem, recv_sem=r_sem, device_id=device, device_id_type=MESH
        )
        copy.start()
        sends.append(copy)

    counter = []

    def spread(source, slot, part, peer):
        index = len(counter)
        counter.append(0)
        send(kv.at[source, part], kv.at[slot, part], ag_s.at[index], ag_r.at[slot, part], {"ctx": peer})

    def arrived(slot, part):
        pltpu.make_async_remote_copy(
            src_ref=kv.at[slot, part], dst_ref=kv.at[slot, part], send_sem=ag_s.at[0], recv_sem=ag_r.at[slot, part],
            device_id={"ctx": other}, device_id_type=MESH,
        ).wait_recv()

    def prepare_keys(start, keys, values):
        count = keys.shape[0]
        kT[:, start:start + count] = keys.T
        vT[0:128, start:start + count] = values.T
        vn[start:start + count, :] = values
        scaled = keys.astype(f32) * LOG2_SCALE
        high = scaled.astype(bf16)
        k2[start:start + count, 0:128] = high
        k2[start:start + count, 128:256] = (scaled - high.astype(f32)).astype(bf16)

    def ready(slot, part):
        prepare_keys(START[slot, part], kv[slot, part, 0], kv[slot, part, 1])

    loads["pk"].wait()
    loads["pv"].wait()
    for part in range(PARTS):
        for owner in range(8):
            rows = slice(owner * PIECE + part * 16, owner * PIECE + part * 16 + 16)
            kv[0, part, 0, owner * 16:owner * 16 + 16, :] = pk_v[rows, :]
            kv[0, part, 1, owner * 16:owner * 16 + 16, :] = pv_v[rows, :]
    pl.semaphore_wait(barrier, 13)
    for part in (1, 2, 0):
        if part == 0:
            spread(0, 6, part, opposite_chip)
        spread(0, 3, part, ahead)
        spread(0, 2, part, behind)
        spread(0, 1, part, other)

    loads["q"].wait()
    loads["seg"].wait()
    loads["sk"].wait()
    loads["sv"].wait()
    loads["do"].wait()
    for head in range(HEADS):
        cols = head_cols(head)
        width = slice(head * 128, (head + 1) * 128)
        q_head, do_head = q_v[:, width], do_v[:, width]
        q_turned = q_head.T
        qT[0:128, cols] = q_turned
        qT[128:256, cols] = q_turned
        dT[:, cols] = do_head.T
        qs[cols, :] = q_head
        ds[cols, :] = do_head
    seg = jnp.broadcast_to(seg_v[...].astype(f32), (TOKENS, TOKENS))
    key_id = lax.broadcasted_iota(jnp.int32, (TOKENS, TOKENS), 0)
    token_id = lax.broadcasted_iota(jnp.int32, (TOKENS, TOKENS), 1)
    bias[...] = jnp.where((seg == seg.T) & (key_id <= token_id), 0.0, -1e30)
    vT[128:144, :] = jnp.where(lax.broadcasted_iota(jnp.int32, (16, KEYS), 0) == 0, 1.0, 0.0).astype(bf16)
    prepare_keys(0, sk_v[...], sv_v[...])
    for part in range(PARTS):
        ready(0, part)

    def before_chunk(chunk):
        for slot, part in ARRIVALS[chunk]:
            if slot == 3:
                arrived(3, part)
                if part > 0:
                    spread(3, 6, part, ahead)
                if part == 2:
                    spread(3, 7, part, ahead_other)
                spread(3, 4, part, other)
            if slot == 2:
                arrived(2, part)
                spread(2, 5, part, other)
            if slot == 6 and part == 0:
                arrived(6, part)
                spread(6, 7, part, other)
        for slot, part in ARRIVALS[chunk]:
            if slot in (1, 4, 5, 7) or (slot, part) == (6, 2):
                arrived(slot, part)
            ready(slot, part)

    steps = [(chunk, head) for chunk in range(len(CHUNKS)) for head in range(HEADS)]
    peak, fade = {}, {}

    def score_strip(index, at, count):
        chunk, head = steps[index]
        start = CHUNKS[chunk][0] + at
        s = dot(k2[start:start + count, :], qT[:, head_cols(head)])
        if chunk == 0 and at < TOKENS:
            s = s + bias[at:at + count, :]
        s_buf[index % 2, at:at + count, :] = s
        part = jnp.max(s.reshape(count // 8, 8, TOKENS), 0)
        peak[index] = part if index not in peak else jnp.maximum(peak[index], part)

    def finish_peak(index):
        chunk, head = steps[index]
        cols = head_cols(head)
        highest = jnp.max(peak[index], 0, keepdims=True)
        if chunk > 0:
            before = top[:, cols]
            highest = jnp.maximum(highest, before)
            fade[index] = jnp.exp2(before - highest)
        top[:, cols] = highest
        tops[chunk:chunk + 1, cols] = highest
        peak[index] = highest

    def weight_strip(index, at, count):
        chunk, head = steps[index]
        start = CHUNKS[chunk][0] + at
        p_buf[start:start + count, head_cols(head)] = jnp.exp2(
            s_buf[index % 2, at:at + count, :] - peak[index]
        ).astype(bf16)

    def gather_values(index):
        chunk, head = steps[index]
        cols = head_cols(head)
        start, count = CHUNKS[chunk]
        found = dot(vT[:, start:start + count], p_buf[start:start + count, cols])
        if chunk > 0:
            total[:, cols] = total[:, cols] * fade[index] + found[128:129]
            acc[:, cols] = acc[:, cols] * fade[index] + found[:128]
        else:
            total[:, cols] = found[128:129]
            acc[:, cols] = found[:128]

    def weight_gradients(index):
        chunk, head = steps[index]
        start, count = CHUNKS[chunk]
        g_buf[start:start + count, head_cols(head)] = dot(vn[start:start + count, :], dT[:, head_cols(head)])

    for at, count in strips(CHUNKS[0][1]):
        score_strip(0, at, count)
    for index in range(len(steps)):
        finish_peak(index)
        now = strips(CHUNKS[steps[index][0]][1])
        later = []
        if index + 1 < len(steps):
            chunk = steps[index + 1][0]
            if chunk != steps[index][0]:
                before_chunk(chunk)
            later = strips(CHUNKS[chunk][1])
        for turn in range(max(len(now), len(later))):
            if turn < len(later):
                score_strip(index + 1, *later[turn])
            if turn < len(now):
                weight_strip(index, *now[turn])
            if turn == 0 and index > 0:
                gather_values(index - 1)
        weight_gradients(index)
        if steps[index] == (4, 1):
            arrived(6, 1)
            spread(6, 7, 1, other)
    gather_values(len(steps) - 1)

    for head in range(HEADS):
        cols = head_cols(head)
        inverse = 1.0 / total[:, cols]
        out = acc[:, cols] * inverse
        delta[:, cols] = jnp.sum(out * dT[:, cols].astype(f32), 0, keepdims=True)
        acc[:, cols] = out
        for chunk in range(len(CHUNKS)):
            factor[chunk:chunk + 1, cols] = jnp.exp2(tops[chunk:chunk + 1, cols] - top[:, cols]) * inverse

    def back(start, count, chunk):
        for head in range(HEADS):
            cols = head_cols(head)
            weights = p_buf[start:start + count, cols] * factor[chunk:chunk + 1, cols].astype(bf16)
            p_buf[start:start + count, cols] = weights
            d_weights = g_buf[start:start + count, cols]
            d_buf[start:start + count, cols] = weights * (d_weights - delta[:, cols]).astype(bf16)
        rows = slice(start, start + count)
        return dot(d_buf[rows, :], qs[...]) * SCALE, dot(p_buf[rows, :], ds[...])

    def back_part(slot, part):
        return back(START[slot, part], PART, CHUNK_OF[slot, part])

    def for_other(index, part, slot):
        dk, dv = back_part(slot, part)
        sib_send[index, part, :, 0:128] = dk.astype(bf16)
        sib_send[index, part, :, 128:256] = dv.astype(bf16)

    def hold(index, part, slot):
        dk, dv = back_part(slot, part)
        keep[index, part, :, 0:128] = dk
        keep[index, part, :, 128:256] = dv

    def to_other(*places):
        for index, part in places:
            landing = LANDING[index]
            send(
                sib_send.at[index, part], sib_recv.at[landing, part], sib_s.at[index, part], sib_r.at[landing, part],
                {"ctx": other},
            )

    def landed(buffer, sems, index, part):
        pltpu.make_async_remote_copy(
            src_ref=buffer.at[index, part], dst_ref=buffer.at[index, part],
            send_sem=sems.at[index, part], recv_sem=sems.at[index, part],
            device_id={"ctx": other}, device_id_type=MESH,
        ).wait_recv()

    def to_chips(*places):
        for index, part in places:
            landed(sib_recv, sib_r, ROW_SENT[index], part)
            if index == 2 and part in RING:
                landed(x_recv, x_r, 0, part)
        for index, part in places:
            row = ROW_SENT[index]
            value = keep[row, part] + sib_recv[row, part].astype(f32)
            if index == 2 and part in RING:
                value = value + x_recv[0, part].astype(f32)
            x_send[index, part] = value.astype(bf16)
        for index, part in places:
            peer = (ahead, behind, ahead, opposite_chip)[index]
            send(x_send.at[index, part], x_recv.at[index, part], x_s.at[index, part], x_r.at[index, part], {"ctx": peer})

    def opposite(part):
        for_other(0, part, 7)
        hold(0, part, 6)

    def sides_other(part):
        for_other(1, part, 4)
        for_other(2, part, 5)

    def sides_same(part):
        hold(2, part, 3)
        hold(1, part, 2)

    def own(part):
        for_other(3, part, 1)
        hold(3, part, 0)

    def exchange(part):
        landed(sib_recv, sib_r, 3, part)
        landed(x_recv, x_r, 1, part)
        landed(x_recv, x_r, 2, part)
        mine = keep[3, part] + sib_recv[3, part].astype(f32)
        mine = mine + x_recv[1, part].astype(f32) + x_recv[2, part].astype(f32)
        if part not in RING:
            landed(x_recv, x_r, 3, part)
            mine = mine + x_recv[3, part].astype(f32)
        keep[3, part] = mine
        for owner in range(8):
            y_send[part, owner] = mine[owner * 16:owner * 16 + 16, :].astype(bf16)
        for step in (4, 3, 5, 2, 6, 1, 7):
            peer = (dp + step) % 8
            send(y_send.at[part, peer], y_recv.at[part, step], y_s.at[part, step], y_r.at[part, step], {"dp": peer})

    def finish(part):
        for step in range(1, 8):
            landed(y_recv, y_r, part, step)
        mine = keep[3, part, pl.ds(pl.multiple_of(dp * 16, 16), 16), :]
        for step in range(1, 8):
            mine = mine + y_recv[part, step].astype(f32)
        dpk_ref[part * 16:part * 16 + 16, :] = mine[:, 0:128]
        dpv_ref[part * 16:part * 16 + 16, :] = mine[:, 128:256]

    def own_keys():
        dk, dv = back(0, TOKENS, 0)
        dsk_ref[...] = dk.astype(bf16)
        dsv_ref[...] = dv.astype(bf16)

    def attended(head):
        out_ref[:, head * 128:(head + 1) * 128] = acc[:, head_cols(head)].T.astype(bf16)

    def queries_gradient(head):
        turned = dot(kT[...], d_buf[:, head_cols(head)]) * SCALE
        dq_ref[:, head * 128:(head + 1) * 128] = turned.T.astype(bf16)

    opposite(0)
    to_other((0, 0))
    opposite(1)
    opposite(2)
    to_other((0, 1), (0, 2))
    to_chips((3, 0))
    sides_other(0)
    sides_same(0)
    to_other((1, 0), (2, 0))
    to_chips((3, 1), (3, 2))
    sides_other(1)
    sides_same(1)
    to_other((1, 1), (2, 1))
    to_chips((1, 0), (2, 0))
    sides_other(2)
    sides_same(2)
    to_other((1, 2), (2, 2))
    to_chips((1, 1), (2, 1))
    own(0)
    own(1)
    to_other((3, 0), (3, 1))
    to_chips((1, 2), (2, 2))
    own(2)
    own_keys()
    to_other((3, 2))
    for head in range(2):
        queries_gradient(head)
    exchange(0)
    for head in range(2, HEADS):
        queries_gradient(head)
    for head in range(HEADS):
        attended(head)
    exchange(1)
    exchange(2)
    for copy in sends:
        copy.wait_send()
    for part in range(PARTS):
        finish(part)


def hand_over(*refs):
    copies = [pltpu.make_async_copy(refs[i], refs[6 + i], refs[12].at[i]) for i in range(6)]
    for copy in copies:
        copy.start()
    for copy in copies:
        copy.wait()


def shards(queries, suffix_keys, suffix_values, pre_keys, pre_values, segments, d_out):
    anywhere = pl.BlockSpec(memory_space=pl.ANY)
    inside = pl.BlockSpec(memory_space=pltpu.VMEM)
    dma = pltpu.SemaphoreType.DMA
    shapes = [
        ((TOKENS, HEADS * HEAD_WIDTH), bf16),
        ((TOKENS, HEADS * HEAD_WIDTH), bf16),
        ((TOKENS, HEAD_WIDTH), bf16),
        ((TOKENS, HEAD_WIDTH), bf16),
        ((PIECE, HEAD_WIDTH), f32),
        ((PIECE, HEAD_WIDTH), f32),
    ]
    out_shape = [jax.ShapeDtypeStruct(shape, dtype) for shape, dtype in shapes]
    results = pl.pallas_call(
        kernel,
        out_shape=[pltpu.VMEM(shape, dtype) for shape, dtype in shapes],
        in_specs=[anywhere] * 7,
        out_specs=[inside] * 6,
        scratch_shapes=[
            pltpu.VMEM((TOKENS, HEADS * HEAD_WIDTH), bf16),
            pltpu.VMEM((TOKENS, HEAD_WIDTH), bf16),
            pltpu.VMEM((TOKENS, HEAD_WIDTH), bf16),
            pltpu.VMEM((OWN, HEAD_WIDTH), bf16),
            pltpu.VMEM((OWN, HEAD_WIDTH), bf16),
            pltpu.VMEM((1, TOKENS), jnp.int32),
            pltpu.VMEM((TOKENS, HEADS * HEAD_WIDTH), bf16),
            pltpu.VMEM((8, PARTS, 2, PART, HEAD_WIDTH), bf16),
            pltpu.VMEM((256, ROWS), bf16),
            pltpu.VMEM((128, ROWS), bf16),
            pltpu.VMEM((ROWS, HEAD_WIDTH), bf16),
            pltpu.VMEM((ROWS, HEAD_WIDTH), bf16),
            pltpu.VMEM((128, KEYS), bf16),
            pltpu.VMEM((144, KEYS), bf16),
            pltpu.VMEM((KEYS, 256), bf16),
            pltpu.VMEM((TOKENS, TOKENS), f32),
            pltpu.VMEM((1, ROWS), f32),
            pltpu.VMEM((1, ROWS), f32),
            pltpu.VMEM((128, ROWS), f32),
            pltpu.VMEM((8, ROWS), f32),
            pltpu.VMEM((1, ROWS), f32),
            pltpu.VMEM((8, ROWS), f32),
            pltpu.VMEM((2, 768, TOKENS), f32),
            pltpu.VMEM((KEYS, ROWS), bf16),
            pltpu.VMEM((KEYS, ROWS), bf16),
            pltpu.VMEM((KEYS, HEAD_WIDTH), bf16),
            pltpu.VMEM((KEYS, ROWS), f32),
            pltpu.VMEM((4, PARTS, PART, 256), f32),
            pltpu.VMEM((4, PARTS, PART, 256), bf16),
            pltpu.VMEM((4, PARTS, PART, 256), bf16),
            pltpu.VMEM((4, PARTS, PART, 256), bf16),
            pltpu.VMEM((4, PARTS, PART, 256), bf16),
            pltpu.VMEM((PARTS, 8, 16, 256), bf16),
            pltpu.VMEM((PARTS, 8, 16, 256), bf16),
            dma((7,)), dma((21,)), dma((8, PARTS)), dma((4, PARTS)), dma((4, PARTS)),
            dma((4, PARTS)), dma((4, PARTS)), dma((PARTS, 8)), dma((PARTS, 8)),
        ],
        compiler_params=pltpu.CompilerParams(
            collective_id=0, has_side_effects=True, vmem_limit_bytes=56 << 20
        ),
    )(queries, suffix_keys, suffix_values, pre_keys, pre_values, segments, d_out)
    return pl.pallas_call(
        hand_over,
        out_shape=out_shape,
        in_specs=[inside] * 6,
        out_specs=[anywhere] * 6,
        scratch_shapes=[dma((6,))],
        compiler_params=pltpu.CompilerParams(vmem_limit_bytes=2 << 20),
    )(*results)


def solution(mesh):
    split = P(("ctx", "dp"), "mp")
    in_specs = (split, split, split, P("ctx", "mp"), P("ctx", "mp"), P(("ctx", "dp"), None), split)
    return jax.shard_map(shards, mesh=mesh, in_specs=in_specs, out_specs=(split,) * 6, check_vma=False)
```
